512 devices in a mesh: bank: 128 (over y, z, core), head: 4 (over x).
Axes of the slice: x: 4, y: 4, z: 16, core: 2. Of those that a mesh axis runs over, the one named last changes fastest.
Arguments:
- inputs: bfloat16 [4096, 768], P('bank'), may hold values from -6 to 6
- positives: bfloat16 [4096, 768], P('bank'), may hold values from -0.21875 to 0.21875
- margins: float32 [4096, 32], P('bank'), may hold values from -6 to 6
- neg_block: int32 [4096, 32], P('bank'), may hold values from 0 to 511, as said below
- neg_row: int32 [4096, 32], P('bank'), may hold values from 0 to 127
- block_home: int32 [512], replicated, may hold values from 0 to 511, as said below
- bank: bfloat16 [65536, 768], P('bank'), may hold values from -0.21875 to 0.21875
- up_weight: bfloat16 [768, 3072], P(None, 'head'), may hold values from -0.21875 to 0.21875
- up_bias: float32 [3072], P('head'), may hold values from -5 to 5
- down_weight: bfloat16 [3072, 768], P('head'), may hold values from -0.109375 to 0.109375
Outputs:
- grad_inputs: bfloat16 [4096, 768], P(('bank', 'head'))
- grad_down: bfloat16 [3072, 768], P('head')
The draws below stay inside these ranges and needn't reach their ends.
Inputs may be any that keep to these rules, and one draw needn't show every extreme that they name: `block_home`: storage position p holds block rows p * 128 to p * 128 + 127 of bank; each position holds one block. `neg_block`: call p // 4, with p the storage position of a negative's block, its owner. Among the 256 pairs of an aligned group of 8 queries, at most 4 have one owner; in every group some owners have exactly 4, and one owner has exactly 4 in every group.
All inputs are finite; a program needn't handle non-finite values.
Results may differ from the reference program's by a relative error of at most 0.02.
Values may be sent and summed in bfloat16 or wider, within the bound.
A program may use at most 64 MiB of HBM per device.

```python
import math
import jax
import jax.numpy as jnp
from jax import lax

D = 768
FF = 3072
NEG = 32
BLOCK_ROWS = 128
Q_DEV = 32
BLOCKS = 512
Q_HEAD = 8
QUERIES = 4096
BLK_OWN = 4
PAIRS = 256
CAP = 4
N_BANK = 128


def shared_home(key):
    return jax.random.permutation(jax.random.fold_in(key, 77), BLOCKS).astype(jnp.int32)


def draw_block_home(key, part):
    placed = shared_home(key)
    return placed


def draw_neg_block(key, part):
    placed = shared_home(key)
    key = jax.random.fold_in(key, 5)
    keys_list = jax.random.split(key, 5)
    groups = QUERIES // Q_HEAD
    owner_ids = jnp.arange(N_BANK, dtype=jnp.int32)
    favour = jax.random.randint(keys_list[0], (N_BANK,), 0, 4)
    star_owner = jax.random.randint(keys_list[1], (), 0, N_BANK)
    jitter = jax.random.randint(keys_list[2], (groups, N_BANK), 0, 4 * N_BANK)
    boost = jnp.where(owner_ids == star_owner, 16 * N_BANK, 0)
    scores = favour[None, :] * (3 * N_BANK) + jitter + boost[None, :]
    scores = scores * N_BANK + owner_ids[None, :]
    ranking = jnp.argsort(-scores, axis=1).astype(jnp.int32)
    hot_count = N_BANK // 4
    pair_ids = jnp.arange(PAIRS, dtype=jnp.int32)
    rank_of_pair = jnp.where(pair_ids < hot_count * CAP, pair_ids // CAP, hot_count + (pair_ids - hot_count * CAP) % (N_BANK - hot_count)).astype(jnp.int32)
    shuffled = jax.vmap(lambda subkey: jax.random.permutation(subkey, rank_of_pair))(jax.random.split(keys_list[3], groups))
    owners = jnp.take_along_axis(ranking, shuffled, axis=1)
    within = jax.random.randint(keys_list[4], (groups, PAIRS), 0, BLK_OWN)
    inverse = jnp.argsort(placed).astype(jnp.int32)
    return inverse[owners * BLK_OWN + within].reshape(QUERIES, NEG).astype(jnp.int32)


def touch_ends(drawn, own_key, smallest, top_value):
    longest = drawn.shape.index(max(drawn.shape))
    spots = []
    for shift in (0, 1):
        where = [jax.random.randint(jax.random.fold_in(own_key, axis), (), 0, length) for axis, length in enumerate(drawn.shape)]
        where[longest] = (where[longest] + shift) % drawn.shape[longest]
        spots.append(tuple(where))
    return drawn.at[spots[0]].set(smallest).at[spots[1]].set(top_value)


def block_levels(key, dims, cuts, low, high):
    level = 1.0
    for position, shards_of in cuts:
        heights = jax.random.uniform(jax.random.fold_in(jax.random.fold_in(key, 6), position), (shards_of,), jnp.float32, low / len(cuts), high / len(cuts))
        level = level * jnp.repeat(jnp.exp(heights), dims[position] // shards_of).reshape((-1,) + (1,) * (len(dims) - 1 - position))
    return level


def normal_values(rng, dims, scale, reach, shards=(), kind=jnp.bfloat16):
    drawn = scale * jax.random.normal(rng, dims, jnp.float32)
    if shards:
        drawn = drawn * block_levels(rng, dims, shards, -0.22, 0.18)
    return jnp.clip(drawn, -reach, reach).astype(kind)


def setup_inputs(seed: int = 0) -> dict:
    key_list = jax.random.split(jax.random.key(seed), 11)
    inputs = normal_values(key_list[0], (QUERIES, D), 1.0, 6.0, ((0, 128),))
    positives = normal_values(key_list[1], (QUERIES, D), D ** -0.5, 0.21875, ((0, 128),))
    margins = normal_values(key_list[2], (QUERIES, NEG), 1.0, 6.0, ((0, 128),), jnp.float32)
    neg_block = draw_neg_block(jax.random.fold_in(key_list[10], 71), 0)
    neg_row = touch_ends(jax.random.randint(key_list[4], (QUERIES, NEG), 0, BLOCK_ROWS), jax.random.fold_in(key_list[4], 1), 0, BLOCK_ROWS - 1).astype(jnp.int32)
    block_home = draw_block_home(jax.random.fold_in(key_list[10], 71), 0)
    bank = normal_values(key_list[6], (BLOCKS * BLOCK_ROWS, D), D ** -0.5, 0.21875, ((0, 128),))
    up_weight = normal_values(key_list[7], (D, FF), D ** -0.5, 0.21875, ((1, 4),))
    up_bias = normal_values(key_list[8], (FF,), 1.0, 5.0, ((0, 4),), jnp.float32)
    down_weight = normal_values(key_list[9], (FF, D), FF ** -0.5, 0.109375, ((0, 4),))
    return {"inputs": inputs, "positives": positives, "margins": margins, "neg_block": neg_block, "neg_row": neg_row, "block_home": block_home, "bank": bank, "up_weight": up_weight, "up_bias": up_bias, "down_weight": down_weight}


def gelu_tanh(values):
    return jax.nn.gelu(values, approximate=True)

def negatives_term(parts, bank):
    embedded, offsets, row_ids, positive = parts
    neighbours = bank[row_ids].astype(jnp.float32)
    scores = jnp.einsum('bd,bjd->bj', embedded.astype(jnp.float32), neighbours)
    residual = offsets.astype(jnp.float32) - scores
    weighted = lax.optimization_barrier((residual[:, :, None] * neighbours).astype(jnp.bfloat16))
    rounded = lax.optimization_barrier(residual.astype(jnp.bfloat16))
    total_weight = lax.optimization_barrier(jnp.sum(rounded.astype(jnp.float32), axis=1))
    return 2.0 * positive.astype(jnp.float32) * total_weight[:, None] - 2.0 * lax.optimization_barrier(jnp.sum(weighted.astype(jnp.float32), axis=1))

def reference(inputs, positives, margins, neg_block, neg_row, block_home, bank, up_weight, up_bias, down_weight):
    pre = jnp.dot(inputs, up_weight, preferred_element_type=jnp.float32) + up_bias.astype(jnp.float32)
    hidden = gelu_tanh(pre).astype(jnp.bfloat16)
    query_emb = inputs.astype(jnp.float32) + jnp.dot(hidden, down_weight, preferred_element_type=jnp.float32)
    embedded = query_emb.astype(jnp.bfloat16)
    positive_score = lax.optimization_barrier(jnp.sum(embedded.astype(jnp.float32) * positives.astype(jnp.float32), axis=1))
    offsets = (positive_score[:, None] - margins.astype(jnp.float32)).astype(jnp.bfloat16)
    row_ids = (block_home[neg_block] * BLOCK_ROWS + neg_row).astype(jnp.int32)
    groups = QUERIES // Q_DEV
    stacked = (embedded.reshape(groups, Q_DEV, D), offsets.reshape(groups, Q_DEV, NEG), row_ids.reshape(groups, Q_DEV, NEG), positives.reshape(groups, Q_DEV, D))
    gradient = lax.map(lambda parts: negatives_term(parts, bank), stacked).reshape(QUERIES, D)
    grad_rounded = gradient.astype(jnp.bfloat16)
    hidden_grad = jnp.dot(grad_rounded, down_weight.T, preferred_element_type=jnp.float32)
    unused, pullback = jax.vjp(gelu_tanh, pre)
    pre_grad = pullback(hidden_grad)[0].astype(jnp.bfloat16)
    grad_inputs = (gradient + jnp.dot(pre_grad, up_weight.T, preferred_element_type=jnp.float32)).astype(jnp.bfloat16)
    summed = lax.dot_general(hidden, grad_rounded, (((0,), (0,)), ((), ())), preferred_element_type=jnp.float32)
    grad_down = (summed / math.sqrt(QUERIES)).astype(jnp.bfloat16)
    return (grad_inputs, grad_down)
```

```python
import functools
import math

import jax
import jax.numpy as jnp
from jax import lax
from jax.experimental import pallas as pl
from jax.experimental.pallas import tpu as pltpu
from jax.sharding import PartitionSpec as P

MESH = pl.DeviceIdType.MESH
F32 = jnp.float32
BF16 = jnp.bfloat16
I32 = jnp.int32
NEG = 32
BLOCK_ROWS = 128
QH = 8
PAIRS = QH * NEG
K0 = math.sqrt(2.0 / math.pi)
K1 = 0.044715


def iota(shape, axis):
    return lax.broadcasted_iota(I32, shape, axis)


def dot(a, b, ca=1, cb=0):
    return lax.dot_general(a, b, (((ca,), (cb,)), ((), ())), preferred_element_type=F32)


def fold(rows):
    w = rows.shape[1] // 2
    return jnp.concatenate([rows[:, :w], rows[:, w:]], axis=0)


def unfold(rows):
    return jnp.concatenate([rows[:QH], rows[QH:]], axis=1)


def kernel(
    dims,
    in_ref, pos_ref, nb_ref, nr_ref, mg_ref, home_ref, bank_ref, up_ref, bias_ref, down_ref,
    gi_ref, gd_ref,
    meta_all, e_all, ps_all, h_all, f_all, gd_all,
    xs, xr, xs2, xr2, xg, in_l, pos_l, dgelu, grad_own,
    pm_sc, row_c, q_c, m_c,
    g_own, g_send, gc_recv, gy_send, gy_recv, gz_send, gz_recv,
    r_own, r_send, rc_recv, ry_send, ry_recv, rz_send, rz_recv,
    g_half, p_sc, pz_recv,
    xsem, zsem, ysem, csem,
):
    nx, ny, nz, nc, cap = dims
    b = lax.axis_index("bank")
    x = lax.axis_index("head")
    c = lax.rem(b, nc)
    z = lax.rem(b // nc, nz)
    y = b // (nc * nz)
    oc = 1 - c
    width = in_ref.shape[1]
    half = width // 2
    hidden_units = up_ref.shape[1]
    rows_own = bank_ref.shape[0]
    homes = home_ref.shape[1]
    gd_pieces = hidden_units // ny // 16
    block = nz

    def bid(yy, zz, cc):
        return (yy * nz + zz) * nc + cc

    def xdev(d):
        return (b, lax.rem(x + d, nx))

    def zdev(d):
        return (bid(y, lax.rem(z + d, nz), c), x)

    def ydev(d):
        return (bid(lax.rem(y + d, ny), z, c), x)

    cdev = (bid(y, z, oc), x)
    g_me = (c * ny + y) * nz + z

    def copy(src, dst, sems, i, dev):
        return pltpu.make_async_remote_copy(
            src_ref=src, dst_ref=dst, send_sem=sems.at[0, i], recv_sem=sems.at[1, i],
            device_id=dev, device_id_type=MESH,
        )

    def zloop(fn):
        def body(d, carry):
            fn(d)
            return carry
        lax.fori_loop(1, nz, body, 0)

    def zcopy(k, d, src, dst):
        return copy(src, dst, zsem, k * nz + d, zdev(d))

    def ycopy(k, d, src, dst):
        return copy(src, dst, ysem, k * ny + d, ydev(d))

    def ccopy(k, j, src, dst):
        return copy(src, dst, csem, k * ny + j, cdev)

    def xcopy(k, d, src, dst):
        return copy(src, dst, xsem, k * nx + d, xdev(d))

    barrier = pltpu.get_barrier_semaphore()
    pl.semaphore_signal(barrier, inc=1, device_id=cdev, device_id_type=MESH)
    for d in range(1, nx):
        pl.semaphore_signal(barrier, inc=1, device_id=xdev(d), device_id_type=MESH)
    for d in range(1, ny):
        pl.semaphore_signal(barrier, inc=1, device_id=ydev(d), device_id_type=MESH)
    zloop(lambda d: pl.semaphore_signal(barrier, inc=1, device_id=zdev(d), device_id_type=MESH))

    home = home_ref[...]
    part = iota((8, homes), 0)
    home8 = jnp.broadcast_to(home, (8, homes))
    table = jnp.where(part == 0, home8 >> 1, jnp.where(part == 1, home8 & 1, 0))
    table = table.astype(F32).astype(BF16)
    for i in range(PAIRS // 128):
        blocks = nb_ref[pl.ds(2 * x + i, 1), :]
        hot = jnp.where(iota((homes, 128), 0) == blocks, 1.0, 0.0).astype(BF16)
        found = dot(table, hot)
        place = 2.0 * found[0:1] + found[1:2]
        ids = place * float(BLOCK_ROWS) + nr_ref[pl.ds(2 * x + i, 1), :].astype(F32)
        meta_all[g_me, :, pl.ds(128 * i, 128)] = ids
        meta_all[g_me, :, pl.ds(PAIRS + 128 * i, 128)] = mg_ref[pl.ds(2 * x + i, 1), :]

    pl.semaphore_wait(barrier, (nx - 1) + (ny - 1) + (nz - 1) + 1)

    def own(ref, n=1):
        return ref.at[pl.ds(g_me, n)]

    zloop(lambda d: zcopy(0, d, own(meta_all), own(meta_all)).start())

    queries = in_ref[...]
    pre = dot(queries, up_ref[...]) + bias_ref[...]
    t = jnp.tanh(K0 * (pre + K1 * (pre * pre * pre)))
    hid = (0.5 * pre * (1.0 + t)).astype(BF16)
    h_all[y, c] = hid
    partial = dot(hid, down_ref[...])
    for i in range(nx):
        xs[i] = fold(partial[QH * i:QH * (i + 1)]).astype(BF16)
    for d in range(1, nx):
        xcopy(0, d, xs.at[lax.rem(x + d, nx)], xr.at[d]).start()
    ccopy(0, 0, h_all.at[y, c], h_all.at[y, c]).start()
    dgelu[...] = 0.5 * (1.0 + t) + 0.5 * pre * (1.0 - t * t) * (K0 * (1.0 + 3.0 * K1 * (pre * pre)))
    inf = queries.astype(F32)
    posf = pos_ref[...].astype(F32)
    for i in range(nx):
        in_l[i] = fold(inf[QH * i:QH * (i + 1)])
        pos_l[i] = fold(posf[QH * i:QH * (i + 1)])

    total = xs[x].astype(F32)
    for d in range(1, nx):
        xcopy(0, d, xs.at[0], xr.at[d]).wait_recv()
        total = total + xr[d].astype(F32)
    emb = (in_l[x] + total).astype(BF16)
    e_all[g_me] = emb
    s16 = jnp.sum(emb.astype(F32) * pos_l[x], axis=1, keepdims=True)
    s8 = s16[:QH] + s16[QH:]
    diag = iota((QH, 128), 0) == iota((QH, 128), 1)
    ps_all[g_me] = jnp.sum(jnp.where(diag, s8, 0.0), axis=0, keepdims=True)

    def send_emb(d):
        zcopy(1, d, own(e_all), own(e_all)).start()
        zcopy(2, d, own(ps_all), own(ps_all)).start()

    zloop(send_emb)

    ccopy(0, 0, h_all.at[y, c], h_all.at[y, oc]).wait_recv()
    for d in range(1, ny):
        ycopy(0, d, h_all.at[y], h_all.at[y]).start()

    zloop(lambda d: zcopy(0, d, own(meta_all), own(meta_all)).wait_recv())

    def ring(ref, cc, yy):
        return ref.at[pl.ds((cc * ny + yy) * nz, nz)]

    def yfrom(d):
        return lax.rem(y + ny - d, ny)

    for d in range(1, ny):
        ycopy(1, d, ring(meta_all, c, y), ring(meta_all, c, y)).start()
    ccopy(1, 0, ring(meta_all, c, y), ring(meta_all, c, y)).start()
    for d in range(1, ny):
        ycopy(1, d, ring(meta_all, c, y), ring(meta_all, c, yfrom(d))).wait_recv()
        ccopy(1, d, ring(meta_all, c, yfrom(d)), ring(meta_all, c, yfrom(d))).start()
    for d in range(ny):
        ccopy(1, d, ring(meta_all, c, y), ring(meta_all, oc, yfrom(d))).wait_recv()

    groups = meta_all.shape[0]
    ids = meta_all[:, 0, pl.ds(0, PAIRS)].astype(I32)
    margins = meta_all[:, 0, pl.ds(PAIRS, PAIRS)]
    owner = ids // rows_own
    local = (ids - owner * rows_own).astype(F32)
    mine = owner == b
    tri = jnp.where(iota((PAIRS, PAIRS), 0) <= iota((PAIRS, PAIRS), 1), 1.0, 0.0).astype(BF16)
    prefix = dot(jnp.where(mine, 1.0, 0.0).astype(BF16), tri)
    pm = jnp.where(mine, prefix, 0.0)
    pm_sc[...] = pm
    q_lane = (iota((groups, PAIRS), 1) // NEG + 1).astype(F32)
    for r in range(cap):
        sel = pm == float(r + 1)
        row_c[r] = jnp.sum(jnp.where(sel, local, 0.0), axis=1, keepdims=True)
        q_c[r] = jnp.sum(jnp.where(sel, q_lane, 0.0), axis=1, keepdims=True)
        m_c[r] = jnp.sum(jnp.where(sel, margins, 0.0), axis=1, keepdims=True)

    def wait_emb(d):
        zcopy(1, d, own(e_all), own(e_all)).wait_recv()
        zcopy(2, d, own(ps_all), own(ps_all)).wait_recv()

    zloop(wait_emb)
    for d in range(1, ny):
        ycopy(2, d, ring(e_all, c, y), ring(e_all, c, y)).start()
        ycopy(3, d, ring(ps_all, c, y), ring(ps_all, c, y)).start()
    ccopy(2, 0, ring(e_all, c, y), ring(e_all, c, y)).start()
    ccopy(3, 0, ring(ps_all, c, y), ring(ps_all, c, y)).start()
    for d in range(1, ny):
        src = yfrom(d)
        ycopy(2, d, ring(e_all, c, y), ring(e_all, c, src)).wait_recv()
        ycopy(3, d, ring(ps_all, c, y), ring(ps_all, c, src)).wait_recv()
        ccopy(2, d, ring(e_all, c, src), ring(e_all, c, src)).start()
        ccopy(3, d, ring(ps_all, c, src), ring(ps_all, c, src)).start()
    for d in range(ny):
        ccopy(2, d, ring(e_all, c, y), ring(e_all, oc, yfrom(d))).wait_recv()
        ccopy(3, d, ring(ps_all, c, y), ring(ps_all, oc, yfrom(d))).wait_recv()

    slots = cap * block
    ind = jnp.where(iota((PAIRS, 128), 0) // NEG == iota((PAIRS, 128), 1), 1.0, 0.0).astype(BF16)

    def score_block(cc, yy):
        first = pl.multiple_of((cc * ny + yy) * nz, nz)
        at = pl.ds(first, block)
        rows = jnp.concatenate([row_c[r, at, :] for r in range(cap)], axis=0)
        qs = jnp.concatenate([q_c[r, at, :] for r in range(cap)], axis=0)
        ms = jnp.concatenate([m_c[r, at, :] for r in range(cap)], axis=0)
        filled = qs > 0.5
        row_i = jnp.where(filled, rows, -1.0).astype(I32)
        hot_row = jnp.where(iota((slots, rows_own), 1) == row_i, 1.0, 0.0).astype(BF16)
        near = dot(hot_row, bank_ref[...])
        ps_rows = ps_all[at, 0, :]
        ps_rep = jnp.concatenate([ps_rows] * cap, axis=0)
        q_i = qs.astype(I32) - 1
        ps = jnp.sum(jnp.where(iota((slots, 128), 1) == q_i, ps_rep, 0.0), axis=1, keepdims=True)
        offs = (ps - ms).astype(BF16).astype(F32)
        group_i = lax.rem(iota((slots, 1), 0), block)
        target = jnp.where(filled, group_i * 16 + q_i, -100)
        target = jnp.concatenate([target, target + QH], axis=0)
        hot_q = jnp.where(iota((2 * slots, block * 16), 1) == target, 1.0, 0.0).astype(BF16)
        embs = dot(hot_q, e_all[at].reshape(block * 16, half))
        score = jnp.sum(
            embs[:slots] * near[:, :half] + embs[slots:] * near[:, half:], axis=1, keepdims=True
        )
        residual = offs - score
        weighted = (residual * near).astype(BF16)
        weighted = jnp.concatenate([weighted[:, :half], weighted[:, half:]], axis=0)
        summed = dot(hot_q, weighted, 0, 0).reshape(block, 16, half)
        rounded = residual.astype(BF16).astype(F32)
        pm_b = pm_sc[at, :]
        per_pair = jnp.zeros((block, PAIRS), F32)
        for r in range(cap):
            per_pair = per_pair + jnp.where(
                pm_b == float(r + 1), rounded[r * block:(r + 1) * block], 0.0
            )
        return summed, dot(per_pair.astype(BF16), ind)

    for d in range(ny):
        yy = lax.rem(y + d, ny)
        summed, rsum = score_block(oc, yy)
        g_send[yy] = summed.astype(BF16)
        r_send[yy, :, 0, :] = rsum
        ccopy(4, d, g_send.at[yy], gc_recv.at[yy]).start()
        ccopy(5, d, r_send.at[yy], rc_recv.at[yy]).start()
    for d in range(ny):
        yy = lax.rem(y + d, ny)
        summed, rsum = score_block(c, yy)
        g_own[yy] = summed
        r_own[yy, :, 0, :] = rsum

    def core_sum(d):
        yy = lax.rem(y + d, ny)
        ccopy(4, d, g_send.at[yy], gc_recv.at[yy]).wait_recv()
        ccopy(5, d, r_send.at[yy], rc_recv.at[yy]).wait_recv()
        return g_own[yy] + gc_recv[yy].astype(F32), r_own[yy] + rc_recv[yy]

    for d in range(1, ny):
        g_sum, r_sum = core_sum(d)
        gy_send[d] = g_sum.astype(BF16)
        ry_send[d] = r_sum
        ycopy(4, d, gy_send.at[d], gy_recv.at[d]).start()
        ycopy(5, d, ry_send.at[d], ry_recv.at[d]).start()
    g_sum, r_sum = core_sum(0)
    for d in range(1, ny):
        ycopy(4, d, gy_send.at[d], gy_recv.at[d]).wait_recv()
        ycopy(5, d, ry_send.at[d], ry_recv.at[d]).wait_recv()
        g_sum = g_sum + gy_recv[d].astype(F32)
        r_sum = r_sum + ry_recv[d]
    g_own[0] = g_sum
    rz_send[...] = r_sum
    gz_send[...] = g_sum.astype(BF16)

    def send_sum(d):
        zz = lax.rem(z + d, nz)
        zcopy(3, d, gz_send.at[zz], gz_recv.at[d]).start()
        zcopy(4, d, rz_send.at[zz], rz_recv.at[d]).start()

    zloop(send_sum)

    def add_sum(d, carry):
        zcopy(3, d, gz_send.at[0], gz_recv.at[d]).wait_recv()
        zcopy(4, d, rz_send.at[0], rz_recv.at[d]).wait_recv()
        return carry[0] + gz_recv[d].astype(F32), carry[1] + rz_recv[d]

    wsum, rsum = lax.fori_loop(1, nz, add_sum, (g_own[0, z], rz_send[z]))
    lane_q = iota((16, 128), 1) == lax.rem(iota((16, 128), 0), QH)
    rcol = jnp.sum(jnp.where(lane_q, rsum, 0.0), axis=1, keepdims=True)
    gradient = 2.0 * pos_l[x] * rcol - 2.0 * wsum
    grad_own[...] = gradient
    xg[x] = gradient.astype(BF16)
    for d in range(1, nx):
        xcopy(1, d, xg.at[x], xg.at[x]).start()
    for d in range(1, nx):
        src = lax.rem(x + nx - d, nx)
        xcopy(1, d, xg.at[x], xg.at[src]).wait_recv()

    pieces = [xg[i].astype(F32) for i in range(nx)]
    top = jnp.concatenate([p[:QH] for p in pieces], axis=0)
    low = jnp.concatenate([p[QH:] for p in pieces], axis=0)
    g_half[0] = top.astype(BF16)
    g_half[1] = low.astype(BF16)
    ccopy(6, 0, g_half.at[oc], f_all.at[y, c]).start()
    f_all[y, c] = g_half[c]
    ccopy(6, 0, g_half.at[oc], f_all.at[y, oc]).wait_recv()
    for d in range(1, ny):
        ycopy(6, d, f_all.at[y], f_all.at[y]).start()

    grad_all = jnp.concatenate([top, low], axis=1).astype(BF16)
    hidden_grad = dot(grad_all, down_ref[...], 1, 1)
    pre_grad = (hidden_grad * dgelu[...]).astype(BF16)
    carried = dot(pre_grad, up_ref[...], 1, 1)
    for i in range(nx):
        xs2[i] = fold(carried[QH * i:QH * (i + 1)]).astype(BF16)
    for d in range(1, nx):
        xcopy(2, d, xs2.at[lax.rem(x + d, nx)], xr2.at[d]).start()

    for d in range(1, ny):
        ycopy(0, d, h_all.at[y], h_all.at[yfrom(d)]).wait_recv()
        ycopy(6, d, f_all.at[y], f_all.at[yfrom(d)]).wait_recv()
    count = ny * nc * nx * QH
    down_sum = dot(
        h_all[...].reshape(count, hidden_units), f_all[...].reshape(count, half), 0, 0
    )
    p_sc[...] = down_sum.astype(BF16).reshape(ny * gd_pieces, 16, half)

    def send_down(d):
        zz = lax.rem(z + d, nz)

        @pl.when(zz < gd_pieces)
        def _():
            zcopy(5, d, p_sc.at[y * gd_pieces + zz], pz_recv.at[d]).start()

    zloop(send_down)
    scale = 1.0 / math.sqrt(nx * QH * ny * nz * nc)

    @pl.when(z < gd_pieces)
    def _():
        def add_down(d, carry):
            zcopy(5, d, p_sc.at[0], pz_recv.at[d]).wait_recv()
            return carry + pz_recv[d].astype(F32)

        acc = lax.fori_loop(1, nz, add_down, p_sc[y * gd_pieces + z].astype(F32))
        gd_all[c, y, z] = (acc * scale).astype(BF16)
        zloop(lambda d: zcopy(6, d, gd_all.at[c, y, z], gd_all.at[c, y, z]).start())

    carry = xs2[x].astype(F32) + grad_own[...]
    for d in range(1, nx):
        xcopy(2, d, xs2.at[0], xr2.at[d]).wait_recv()
        carry = carry + xr2[d].astype(F32)
    gi_ref[...] = unfold(carry).astype(BF16)

    def wait_down(d):
        zz = lax.rem(z + nz - d, nz)

        @pl.when(zz < gd_pieces)
        def _():
            zcopy(6, d, gd_all.at[c, y, 0], gd_all.at[c, y, zz]).wait_recv()

    zloop(wait_down)
    for d in range(1, ny):
        ycopy(7, d, gd_all.at[c, y], gd_all.at[c, y]).start()
    ccopy(7, 0, gd_all.at[c, y], gd_all.at[c, y]).start()
    for d in range(1, ny):
        src = yfrom(d)
        ycopy(7, d, gd_all.at[c, y], gd_all.at[c, src]).wait_recv()
        ccopy(7, d, gd_all.at[c, src], gd_all.at[c, src]).start()
    for d in range(ny):
        ccopy(7, d, gd_all.at[c, y], gd_all.at[oc, yfrom(d)]).wait_recv()
    for i in range(nc):
        gd_ref[:, half * i:half * (i + 1)] = gd_all[i].reshape(hidden_units, half)

    def sent(d):
        zz = lax.rem(z + d, nz)
        zcopy(0, d, own(meta_all), own(meta_all)).wait_send()
        zcopy(1, d, own(e_all), own(e_all)).wait_send()
        zcopy(2, d, own(ps_all), own(ps_all)).wait_send()
        zcopy(3, d, gz_send.at[0], gz_recv.at[d]).wait_send()
        zcopy(4, d, rz_send.at[0], rz_recv.at[d]).wait_send()

        @pl.when(zz < gd_pieces)
        def _():
            zcopy(5, d, p_sc.at[0], pz_recv.at[d]).wait_send()

        @pl.when(z < gd_pieces)
        def _():
            zcopy(6, d, gd_all.at[c, y, z], gd_all.at[c, y, z]).wait_send()

    zloop(sent)
    for d in range(1, nx):
        xcopy(0, d, xs.at[0], xr.at[d]).wait_send()
        xcopy(1, d, xg.at[x], xg.at[x]).wait_send()
        xcopy(2, d, xs2.at[0], xr2.at[d]).wait_send()
    for d in range(1, ny):
        ycopy(0, d, h_all.at[y], h_all.at[y]).wait_send()
        ycopy(1, d, ring(meta_all, c, y), ring(meta_all, c, y)).wait_send()
        ycopy(2, d, ring(e_all, c, y), ring(e_all, c, y)).wait_send()
        ycopy(3, d, ring(ps_all, c, y), ring(ps_all, c, y)).wait_send()
        ycopy(4, d, gy_send.at[d], gy_recv.at[d]).wait_send()
        ycopy(5, d, ry_send.at[d], ry_recv.at[d]).wait_send()
        ycopy(6, d, f_all.at[y], f_all.at[y]).wait_send()
        ycopy(7, d, gd_all.at[c, y], gd_all.at[c, y]).wait_send()
    ccopy(0, 0, h_all.at[y, c], h_all.at[y, c]).wait_send()
    ccopy(6, 0, g_half.at[oc], f_all.at[y, c]).wait_send()
    for d in range(ny):
        ccopy(1, d, ring(meta_all, c, y), ring(meta_all, c, y)).wait_send()
        ccopy(2, d, ring(e_all, c, y), ring(e_all, c, y)).wait_send()
        ccopy(3, d, ring(ps_all, c, y), ring(ps_all, c, y)).wait_send()
        ccopy(4, d, g_send.at[0], gc_recv.at[0]).wait_send()
        ccopy(5, d, r_send.at[0], rc_recv.at[0]).wait_send()
        ccopy(7, d, gd_all.at[c, y], gd_all.at[c, y]).wait_send()


def on_device(
    dims, inputs, positives, margins, neg_block, neg_row, block_home, bank, up_weight, up_bias,
    down_weight,
):
    nx, ny, nz, nc, cap = dims
    width = inputs.shape[1]
    half = width // 2
    units = up_weight.shape[1]
    queries = inputs.shape[0]
    groups = ny * nz * nc
    gd_pieces = units // ny // 16
    flat = (queries * NEG // 128, 128)
    V = pltpu.VMEM
    scratch = [
        V((groups, 1, 2 * PAIRS), F32),
        V((groups, 16, half), BF16),
        V((groups, 1, 128), F32),
        V((ny, nc, queries, units), BF16),
        V((ny, nc, queries, half), BF16),
        V((nc, ny, gd_pieces, 16, half), BF16),
        V((nx, 16, half), BF16),
        V((nx, 16, half), BF16),
        V((nx, 16, half), BF16),
        V((nx, 16, half), BF16),
        V((nx, 16, half), BF16),
        V((nx, 16, half), F32),
        V((nx, 16, half), F32),
        V((queries, units), F32),
        V((16, half), F32),
        V((groups, PAIRS), F32),
        V((cap, groups, 1), F32),
        V((cap, groups, 1), F32),
        V((cap, groups, 1), F32),
        V((ny, nz, 16, half), F32),
        V((ny, nz, 16, half), BF16),
        V((ny, nz, 16, half), BF16),
        V((ny, nz, 16, half), BF16),
        V((ny, nz, 16, half), BF16),
        V((nz, 16, half), BF16),
        V((nz, 16, half), BF16),
        V((ny, nz, 1, 128), F32),
        V((ny, nz, 1, 128), F32),
        V((ny, nz, 1, 128), F32),
        V((ny, nz, 1, 128), F32),
        V((ny, nz, 1, 128), F32),
        V((nz, 1, 128), F32),
        V((nz, 1, 128), F32),
        V((nc, queries, half), BF16),
        V((ny * gd_pieces, 16, half), BF16),
        V((nz, 16, half), BF16),
        pltpu.SemaphoreType.DMA((2, 3 * nx)),
        pltpu.SemaphoreType.DMA((2, 7 * nz)),
        pltpu.SemaphoreType.DMA((2, 8 * ny)),
        pltpu.SemaphoreType.DMA((2, 8 * ny)),
    ]
    vmem = pl.BlockSpec(memory_space=pltpu.VMEM)
    return pl.pallas_call(
        functools.partial(kernel, dims),
        out_shape=(
            jax.ShapeDtypeStruct((QH, width), BF16),
            jax.ShapeDtypeStruct((units, width), BF16),
        ),
        in_specs=[vmem] * 10,
        out_specs=(vmem, vmem),
        scratch_shapes=scratch,
        compiler_params=pltpu.CompilerParams(
            collective_id=0, has_side_effects=True, vmem_limit_bytes=40 * 1024 * 1024
        ),
        cost_estimate=pl.CostEstimate(
            flops=4_000_000_000, bytes_accessed=6_000_000, transcendentals=30_000
        ),
    )(
        inputs, positives, neg_block.reshape(flat), neg_row.reshape(flat), margins.reshape(flat),
        block_home.reshape(1, -1), bank, up_weight, up_bias.reshape(1, -1), down_weight,
    )


def solution(mesh, ny=4, nc=2, cap=4):
    nx = mesh.shape["head"]
    nz = mesh.shape["bank"] // (ny * nc)
    return jax.shard_map(
        functools.partial(on_device, (nx, ny, nz, nc, cap)),
        mesh=mesh,
        in_specs=(
            P("bank", None),
            P("bank", None),
            P("bank", None),
            P("bank", None),
            P("bank", None),
            P(),
            P("bank", None),
            P(None, "head"),
            P("head"),
            P("head", None),
        ),
        out_specs=(P(("bank", "head"), None), P("head", None)),
        check_vma=False,
    )
```

```python
import functools
import math

import jax
import jax.numpy as jnp
from jax import lax
from jax.experimental import pallas as pl
from jax.experimental.pallas import tpu as pltpu
from jax.sharding import PartitionSpec as P

MESH = pl.DeviceIdType.MESH
F32 = jnp.float32
BF16 = jnp.bfloat16
I32 = jnp.int32
NEG = 32
BLOCK_ROWS = 128
QH = 8
PAIRS = QH * NEG
K0 = math.sqrt(2.0 / math.pi)
K1 = 0.044715


def iota(shape, axis):
    return lax.broadcasted_iota(I32, shape, axis)


def dot(a, b, ca=1, cb=0):
    return lax.dot_general(a, b, (((ca,), (cb,)), ((), ())), preferred_element_type=F32)


def fold(rows):
    w = rows.shape[1] // 2
    return jnp.concatenate([rows[:, :w], rows[:, w:]], axis=0)


def unfold(rows):
    return jnp.concatenate([rows[:QH], rows[QH:]], axis=1)


def kernel(
    dims,
    in_hbm, pos_hbm, nb_hbm, nr_hbm, mg_hbm, home_hbm, bank_hbm, up_hbm, bias_hbm, down_hbm,
    gi_ref, gd_ref,
    in_ref, pos_ref, nb_ref, nr_ref, mg_ref, home_ref, bank_ref, up_ref, bias_ref, down_ref,
    meta_all, e_all, ps_all, h_all, f_all, gd_all,
    xs, xr, xs2, xr2, xg, in_l, pos_l, dgelu,
    pm_sc, near_sc, q_sc, m_sc,
    g_own, g_send, gc_recv, gy_send, gy_recv, gz_send, gz_recv,
    r_own, r_send, rc_recv, ry_send, ry_recv, rz_send, rz_recv,
    p_sc, pz_recv,
    lsem, xsem, zsem, ysem, csem,
):
    nx, ny, nz, nc, cap = dims
    per = min(4, nz)
    chunks = nz // per
    rings = ny * per
    block = nc * rings
    slots = cap * block
    b = lax.axis_index("bank")
    x = lax.axis_index("head")
    c = lax.rem(b, nc)
    z = lax.rem(b // nc, nz)
    y = b // (nc * nz)
    oc = 1 - c
    width = in_ref.shape[1]
    half = width // 2
    units = up_ref.shape[1]
    rows_own = bank_ref.shape[0]
    homes = home_ref.shape[1]
    gd_pieces = units // ny // 16
    offs = [(s + 1) // 2 if s % 2 else -(s // 2) for s in range(nz)]

    def bid(yy, zz, cc):
        return (yy * nz + zz) * nc + cc

    def zat(off):
        return lax.rem(z + (off + nz), nz)

    def xdev(d):
        return (b, lax.rem(x + d, nx))

    def xcdev(d):
        return (bid(y, z, oc), lax.rem(x + d, nx))

    def zdev(off):
        return (bid(y, zat(off), c), x)

    def ydev(d):
        return (bid(lax.rem(y + d, ny), z, c), x)

    cdev = xcdev(0)
    unsent = []

    def copy(src, dst, sems, i, dev):
        return pltpu.make_async_remote_copy(
            src_ref=src, dst_ref=dst, send_sem=sems.at[0, i], recv_sem=sems.at[1, i],
            device_id=dev, device_id_type=MESH,
        )

    def start(cp, when=None):
        if when is None:
            cp.start()
        else:
            pl.when(when)(cp.start)
        unsent.append((cp, when))

    def zcopy(k, s, off, src, dst):
        return copy(src, dst, zsem, k * nz + s, zdev(off))

    def ycopy(k, d, src, dst):
        return copy(src, dst, ysem, k * ny + d, ydev(d))

    def ccopy(k, src, dst):
        return copy(src, dst, csem, k, cdev)

    def xcopy(k, d, src, dst):
        return copy(src, dst, xsem, k * nx + d, xdev(d))

    pairs = [
        (nb_hbm, nb_ref), (nr_hbm, nr_ref), (mg_hbm, mg_ref), (home_hbm, home_ref),
        (in_hbm, in_ref), (up_hbm, up_ref), (bias_hbm, bias_ref), (down_hbm, down_ref),
        (pos_hbm, pos_ref), (bank_hbm, bank_ref),
    ]
    loads = [pltpu.make_async_copy(src, dst, lsem.at[i]) for i, (src, dst) in enumerate(pairs)]
    for cp in loads:
        cp.start()

    barrier = pltpu.get_barrier_semaphore()
    greet = [xcdev(d) for d in range(nx)] + [xdev(d) for d in range(1, nx)]
    greet += [ydev(d) for d in range(1, ny)] + [zdev(o) for o in offs[1:]]
    for dev in greet:
        pl.semaphore_signal(barrier, inc=1, device_id=dev, device_id_type=MESH)

    for cp in loads[:4]:
        cp.wait()
    mine8 = pl.ds(pl.multiple_of(x * QH, QH), QH)
    lanes = 128 // NEG

    def row_of(rows, i):
        return jnp.concatenate([rows[lanes * i + k:lanes * i + k + 1] for k in range(lanes)], axis=1)

    home = home_ref[...]
    part = iota((8, homes), 0)
    home8 = jnp.broadcast_to(home, (8, homes))
    table = jnp.where(part == 0, home8 >> 1, jnp.where(part == 1, home8 & 1, 0))
    table = table.astype(F32).astype(BF16)
    nb8, nr8, mg8 = nb_ref[mine8, :], nr_ref[mine8, :], mg_ref[mine8, :]
    for i in range(PAIRS // 128):
        hot = jnp.where(iota((homes, 128), 0) == row_of(nb8, i), 1.0, 0.0).astype(BF16)
        found = dot(table, hot)
        place = 2.0 * found[0:1] + found[1:2]
        ids = place * float(BLOCK_ROWS) + row_of(nr8, i).astype(F32)
        meta_all[0, 0, :, pl.ds(128 * i, 128)] = ids
        meta_all[0, 0, :, pl.ds(PAIRS + 128 * i, 128)] = row_of(mg8, i)

    pl.semaphore_wait(barrier, len(greet))

    far_first = list(range(nz - 1, 0, -1))

    def zgather(k, s, ref):
        return zcopy(k, s, -offs[s], ref.at[0, pl.ds(0, 1)], ref.at[s // per, pl.ds(s % per, 1)])

    for s in far_first:
        start(zgather(0, s, meta_all))

    for cp in loads[4:8]:
        cp.wait()
    queries = in_ref[...]
    pre = dot(queries, up_ref[...]) + bias_ref[...]
    t = jnp.tanh(K0 * (pre + K1 * (pre * pre * pre)))
    hid = (0.5 * pre * (1.0 + t)).astype(BF16)
    h_all[0, 0] = hid
    partial = dot(hid, down_ref[...])
    for i in range(nx):
        xs[i] = fold(partial[QH * i:QH * (i + 1)]).astype(BF16)
    for d in range(1, nx):
        start(xcopy(0, d, xs.at[lax.rem(x + d, nx)], xr.at[d]))
    start(ccopy(0, h_all.at[0, 0], h_all.at[0, 1]))
    dgelu[...] = 0.5 * (1.0 + t) + 0.5 * pre * (1.0 - t * t) * (K0 * (1.0 + 3.0 * K1 * (pre * pre)))
    inf = queries.astype(F32)
    loads[8].wait()
    posf = pos_ref[...].astype(F32)
    for i in range(nx):
        in_l[i] = fold(inf[QH * i:QH * (i + 1)])
        pos_l[i] = fold(posf[QH * i:QH * (i + 1)])

    total = xs[x].astype(F32)
    for d in range(1, nx):
        xcopy(0, d, xs.at[0], xr.at[d]).wait_recv()
        total = total + xr[d].astype(F32)
    emb = (in_l[x] + total).astype(BF16)
    e_all[0, 0] = emb
    s16 = jnp.sum(emb.astype(F32) * pos_l[x], axis=1, keepdims=True)
    s8 = s16[:QH] + s16[QH:]
    diag = iota((QH, 128), 0) == iota((QH, 128), 1)
    ps_all[0, 0] = jnp.sum(jnp.where(diag, s8, 0.0), axis=0, keepdims=True)
    for s in far_first:
        start(zgather(1, s, e_all))
        start(zgather(2, s, ps_all))

    def near_ring(ref, k, d=0):
        return ref.at[k, pl.ds(d * per, per)]

    def emb_z(k):
        for s in range(max(1, k * per), (k + 1) * per):
            zgather(1, s, e_all).wait_recv()
            zgather(2, s, ps_all).wait_recv()
        for d in range(1, ny):
            start(ycopy(2 + k, d, near_ring(e_all, k), near_ring(e_all, k, ny - d)))
            start(ycopy(6 + k, d, near_ring(ps_all, k), near_ring(ps_all, k, ny - d)))

    def emb_y(k):
        for d in range(1, ny):
            ycopy(2 + k, d, near_ring(e_all, k), near_ring(e_all, k, ny - d)).wait_recv()
            ycopy(6 + k, d, near_ring(ps_all, k), near_ring(ps_all, k, ny - d)).wait_recv()
        start(emb_core(2 + k, e_all, k))
        start(emb_core(6 + k, ps_all, k))

    def emb_core(i, ref, k):
        return ccopy(i, ref.at[k, pl.ds(0, rings)], ref.at[k, pl.ds(rings, rings)])

    for s in range(1, nz):
        zgather(0, s, meta_all).wait_recv()

    def meta_y(d):
        return ycopy(
            1, d, meta_all.at[:, pl.ds(0, per)], meta_all.at[:, pl.ds((ny - d) * per, per)]
        )

    for d in range(1, ny):
        start(meta_y(d))
    ccopy(0, h_all.at[0, 0], h_all.at[0, 1]).wait_recv()
    for d in range(1, ny):
        meta_y(d).wait_recv()
    meta_c = ccopy(1, meta_all.at[:, pl.ds(0, rings)], meta_all.at[:, pl.ds(rings, rings)])
    start(meta_c)
    emb_z(0)
    meta_c.wait_recv()
    loads[9].wait()

    tri = jnp.where(iota((PAIRS, PAIRS), 0) <= iota((PAIRS, PAIRS), 1), 1.0, 0.0).astype(BF16)
    q_lane = (iota((block, PAIRS), 1) // NEG + 1).astype(F32)
    for k in range(chunks):
        ids = meta_all[k, :, 0, pl.ds(0, PAIRS)].astype(I32)
        margins = meta_all[k, :, 0, pl.ds(PAIRS, PAIRS)]
        owner = ids // rows_own
        local = (ids - owner * rows_own).astype(F32)
        mine = owner == b
        prefix = dot(jnp.where(mine, 1.0, 0.0).astype(BF16), tri)
        pm = jnp.where(mine, prefix, 0.0)
        pm_sc[k] = pm
        rows, qs, ms = [], [], []
        for r in range(cap):
            sel = pm == float(r + 1)
            rows.append(jnp.sum(jnp.where(sel, local, 0.0), axis=1, keepdims=True))
            qs.append(jnp.sum(jnp.where(sel, q_lane, 0.0), axis=1, keepdims=True))
            ms.append(jnp.sum(jnp.where(sel, margins, 0.0), axis=1, keepdims=True))
        rows, qs = jnp.concatenate(rows, axis=0), jnp.concatenate(qs, axis=0)
        q_sc[k] = qs
        m_sc[k] = jnp.concatenate(ms, axis=0)
        row_i = jnp.where(qs > 0.5, rows, -1.0).astype(I32)
        hot_row = jnp.where(iota((slots, rows_own), 1) == row_i, 1.0, 0.0).astype(BF16)
        near_sc[k] = dot(hot_row, bank_ref[...]).astype(BF16)

    ind = jnp.where(iota((PAIRS, 128), 0) // NEG == iota((PAIRS, 128), 1), 1.0, 0.0).astype(BF16)

    def score(k):
        emb_core(2 + k, e_all, k).wait_recv()
        emb_core(6 + k, ps_all, k).wait_recv()
        qs = q_sc[k]
        q_i = qs.astype(I32) - 1
        ps_rep = jnp.concatenate([ps_all[k, :, 0, :]] * cap, axis=0)
        ps = jnp.sum(jnp.where(iota((slots, 128), 1) == q_i, ps_rep, 0.0), axis=1, keepdims=True)
        offsets = (ps - m_sc[k]).astype(BF16).astype(F32)
        group_i = lax.rem(iota((slots, 1), 0), block)
        target = jnp.where(qs > 0.5, group_i * 16 + q_i, -100)
        target = jnp.concatenate([target, target + QH], axis=0)
        hot_q = jnp.where(iota((2 * slots, block * 16), 1) == target, 1.0, 0.0).astype(BF16)
        embs = dot(hot_q, e_all[k].reshape(block * 16, half))
        near = near_sc[k].astype(F32)
        found = jnp.sum(
            embs[:slots] * near[:, :half] + embs[slots:] * near[:, half:], axis=1, keepdims=True
        )
        residual = offsets - found
        weighted = (residual * near).astype(BF16)
        weighted = jnp.concatenate([weighted[:, :half], weighted[:, half:]], axis=0)
        summed = dot(hot_q, weighted, 0, 0).reshape(block, 16, half)
        rounded = residual.astype(BF16).astype(F32)
        pm = pm_sc[k]
        per_pair = jnp.zeros((block, PAIRS), F32)
        for r in range(cap):
            per_pair = per_pair + jnp.where(
                pm == float(r + 1), rounded[r * block:(r + 1) * block], 0.0
            )
        rsum = dot(per_pair.astype(BF16), ind)
        g_send[k] = summed[rings:].astype(BF16)
        r_send[k, :, 0, :] = rsum[rings:]
        start(ccopy(10 + k, g_send.at[k], gc_recv.at[k]))
        start(ccopy(14 + k, r_send.at[k], rc_recv.at[k]))
        g_own[k] = summed[:rings]
        r_own[k, :, 0, :] = rsum[:rings]

    def sum_core(k):
        ccopy(10 + k, g_send.at[k], gc_recv.at[k]).wait_recv()
        ccopy(14 + k, r_send.at[k], rc_recv.at[k]).wait_recv()
        for d in list(range(1, ny)) + [0]:
            at = pl.ds(d * per, per)
            g_sum = g_own[k, at] + gc_recv[k, at].astype(F32)
            r_sum = r_own[k, at] + rc_recv[k, at]
            if d:
                gy_send[k, d] = g_sum.astype(BF16)
                ry_send[k, d] = r_sum
                start(ycopy(10 + k, d, gy_send.at[k, d], gy_recv.at[k, d]))
                start(ycopy(14 + k, d, ry_send.at[k, d], ry_recv.at[k, d]))
            else:
                g_own[k, at] = g_sum
                r_own[k, at] = r_sum

    def sum_y(k):
        g_sum = g_own[k, pl.ds(0, per)]
        r_sum = r_own[k, pl.ds(0, per)]
        for d in range(1, ny):
            ycopy(10 + k, d, gy_send.at[k, d], gy_recv.at[k, d]).wait_recv()
            ycopy(14 + k, d, ry_send.at[k, d], ry_recv.at[k, d]).wait_recv()
            g_sum = g_sum + gy_recv[k, d].astype(F32)
            r_sum = r_sum + ry_recv[k, d]
        gz_send[k] = g_sum.astype(BF16)
        rz_send[k] = r_sum
        if k == 0:
            g_own[0, 0] = g_sum[0]
        for s in range((k + 1) * per - 1, max(1, k * per) - 1, -1):
            start(zcopy(3, s, offs[s], gz_send.at[k, s % per], gz_recv.at[s]))
            start(zcopy(4, s, offs[s], rz_send.at[k, s % per], rz_recv.at[s]))

    def hidden_y():
        for d in range(1, ny):
            start(ycopy(0, d, h_all.at[0], h_all.at[ny - d]))

    stages = [emb_z, emb_y, score, sum_core, sum_y]
    lag = [0, 1, 2, 3, 4]
    for step in range(1, chunks + len(stages) - 1):
        for stage, late in zip(stages, lag):
            if 0 <= step - late < chunks:
                stage(step - late)
        if step == chunks:
            hidden_y()
    if chunks + len(stages) - 2 < chunks:
        hidden_y()

    wsum = g_own[0, 0]
    rsum = rz_send[0, 0]
    for s in range(1, nz):
        zcopy(3, s, offs[s], gz_send.at[0, 0], gz_recv.at[s]).wait_recv()
        zcopy(4, s, offs[s], rz_send.at[0, 0], rz_recv.at[s]).wait_recv()
        wsum = wsum + gz_recv[s].astype(F32)
        rsum = rsum + rz_recv[s]
    lane_q = iota((16, 128), 1) == lax.rem(iota((16, 128), 0), QH)
    rcol = jnp.sum(jnp.where(lane_q, rsum, 0.0), axis=1, keepdims=True)
    gradient = 2.0 * pos_l[x] * rcol - 2.0 * wsum
    xg[0, x] = gradient.astype(BF16)
    for d in range(1, nx):
        start(xcopy(1, d, xg.at[0, x], xg.at[0, x]))
    for d in range(nx):
        start(copy(xg.at[0, x], xg.at[1, x], xsem, 3 * nx + d, xcdev(d)))
    for d in range(nx):
        src = lax.rem(x + nx - d, nx)
        if d:
            xcopy(1, d, xg.at[0, x], xg.at[0, src]).wait_recv()
        copy(xg.at[0, x], xg.at[1, src], xsem, 3 * nx + d, xcdev(d)).wait_recv()

    def halves(cr):
        pieces = [xg[cr, i].astype(F32) for i in range(nx)]
        top = jnp.concatenate([p[:QH] for p in pieces], axis=0)
        low = jnp.concatenate([p[QH:] for p in pieces], axis=0)
        f_all[0, cr] = jnp.where(c == 0, top, low).astype(BF16)
        return top, low

    top, low = halves(0)
    halves(1)
    for d in range(1, ny):
        start(ycopy(18, d, f_all.at[0], f_all.at[ny - d]))

    grad_all = jnp.concatenate([top, low], axis=1).astype(BF16)
    hidden_grad = dot(grad_all, down_ref[...], 1, 1)
    pre_grad = (hidden_grad * dgelu[...]).astype(BF16)
    carried = dot(pre_grad, up_ref[...], 1, 1)
    for i in range(nx):
        xs2[i] = fold(carried[QH * i:QH * (i + 1)]).astype(BF16)
    for d in range(1, nx):
        start(xcopy(2, d, xs2.at[lax.rem(x + d, nx)], xr2.at[d]))

    for d in range(1, ny):
        ycopy(0, d, h_all.at[0], h_all.at[ny - d]).wait_recv()
        ycopy(18, d, f_all.at[0], f_all.at[ny - d]).wait_recv()
    count = ny * nc * nx * QH
    down_sum = dot(h_all[...].reshape(count, units), f_all[...].reshape(count, half), 0, 0)
    p_sc[...] = down_sum.astype(BF16).reshape(ny * gd_pieces, 16, half)
    for s in far_first:
        zz = zat(offs[s])
        piece = p_sc.at[y * gd_pieces + jnp.minimum(zz, gd_pieces - 1)]
        start(zcopy(5, s, offs[s], piece, pz_recv.at[s]), zz < gd_pieces)

    carry = xs2[x].astype(F32) + gradient
    for d in range(1, nx):
        xcopy(2, d, xs2.at[0], xr2.at[d]).wait_recv()
        carry = carry + xr2[d].astype(F32)
    gi_ref[...] = unfold(carry).astype(BF16)

    busy = z < gd_pieces
    scale = 1.0 / math.sqrt(nx * QH * ny * nz * nc)

    @pl.when(busy)
    def _():
        acc = p_sc[y * gd_pieces + jnp.minimum(z, gd_pieces - 1)].astype(F32)
        for s in range(1, nz):
            zcopy(5, s, offs[s], p_sc.at[0], pz_recv.at[s]).wait_recv()
            acc = acc + pz_recv[s].astype(F32)
        gd_all[0, 0] = (acc * scale).astype(BF16)

    def zlast(s):
        return zgather(6, s, gd_all)

    for s in far_first:
        start(zlast(s), busy)

    def last_z(k):
        for s in range(max(1, k * per), (k + 1) * per):
            pl.when(zat(offs[s]) < gd_pieces)(zlast(s).wait_recv)
        for d in range(1, ny):
            start(ycopy(19 + k, d, near_ring(gd_all, k), near_ring(gd_all, k, ny - d)))

    def last_y(k):
        for d in range(1, ny):
            ycopy(19 + k, d, near_ring(gd_all, k), near_ring(gd_all, k, ny - d)).wait_recv()
        start(emb_core(18 + k, gd_all, k))
        put(k, 0)

    def put(k, cr):
        at = c if cr == 0 else oc
        for s in range(per):
            zz = zat(offs[k * per + s])

            @pl.when(zz < gd_pieces)
            def _():
                for d in range(ny):
                    yy = lax.rem(y + d, ny)
                    row = pl.multiple_of((yy * gd_pieces + zz) * 16, 16)
                    col = pl.multiple_of(at * half, 128)
                    gd_ref[pl.ds(row, 16), pl.ds(col, half)] = gd_all[k, cr * rings + d * per + s]

    def last_core(k):
        emb_core(18 + k, gd_all, k).wait_recv()
        put(k, 1)

    stages = [last_z, last_y, last_core]
    for step in range(chunks + len(stages) - 1):
        for late, stage in enumerate(stages):
            if 0 <= step - late < chunks:
                stage(step - late)

    for cp, when in unsent:
        if when is None:
            cp.wait_send()
        else:
            pl.when(when)(cp.wait_send)


def on_device(
    dims, inputs, positives, margins, neg_block, neg_row, block_home, bank, up_weight, up_bias,
    down_weight,
):
    nx, ny, nz, nc, cap = dims
    width = inputs.shape[1]
    half = width // 2
    units = up_weight.shape[1]
    queries = inputs.shape[0]
    per = min(4, nz)
    chunks = nz // per
    rings = ny * per
    block = nc * rings
    slots = cap * block
    gd_pieces = units // ny // 16
    V = pltpu.VMEM
    args = (
        inputs, positives, neg_block, neg_row, margins, block_home.reshape(1, -1), bank,
        up_weight, up_bias.reshape(1, -1), down_weight,
    )
    scratch = [V(a.shape, a.dtype) for a in args] + [
        V((chunks, block, 1, 2 * PAIRS), F32),
        V((chunks, block, 16, half), BF16),
        V((chunks, block, 1, 128), F32),
        V((ny, nc, queries, units), BF16),
        V((ny, nc, queries, half), BF16),
        V((chunks, block, 16, half), BF16),
        V((nx, 16, half), BF16),
        V((nx, 16, half), BF16),
        V((nx, 16, half), BF16),
        V((nx, 16, half), BF16),
        V((nc, nx, 16, half), BF16),
        V((nx, 16, half), F32),
        V((nx, 16, half), F32),
        V((queries, units), F32),
        V((chunks, block, PAIRS), F32),
        V((chunks, slots, width), BF16),
        V((chunks, slots, 1), F32),
        V((chunks, slots, 1), F32),
        V((chunks, rings, 16, half), F32),
        V((chunks, rings, 16, half), BF16),
        V((chunks, rings, 16, half), BF16),
        V((chunks, ny, per, 16, half), BF16),
        V((chunks, ny, per, 16, half), BF16),
        V((chunks, per, 16, half), BF16),
        V((nz, 16, half), BF16),
        V((chunks, rings, 1, 128), F32),
        V((chunks, rings, 1, 128), F32),
        V((chunks, rings, 1, 128), F32),
        V((chunks, ny, per, 1, 128), F32),
        V((chunks, ny, per, 1, 128), F32),
        V((chunks, per, 1, 128), F32),
        V((nz, 1, 128), F32),
        V((ny * gd_pieces, 16, half), BF16),
        V((nz, 16, half), BF16),
        pltpu.SemaphoreType.DMA((len(args),)),
        pltpu.SemaphoreType.DMA((2, 4 * nx)),
        pltpu.SemaphoreType.DMA((2, 7 * nz)),
        pltpu.SemaphoreType.DMA((2, 23 * ny)),
        pltpu.SemaphoreType.DMA((2, 22)),
    ]
    vmem = pl.BlockSpec(memory_space=pltpu.VMEM)
    return pl.pallas_call(
        functools.partial(kernel, dims),
        out_shape=(
            jax.ShapeDtypeStruct((QH, width), BF16),
            jax.ShapeDtypeStruct((units, width), BF16),
        ),
        in_specs=[pl.BlockSpec(memory_space=pltpu.HBM)] * len(args),
        out_specs=(vmem, vmem),
        scratch_shapes=scratch,
        compiler_params=pltpu.CompilerParams(
            collective_id=0, has_side_effects=True, vmem_limit_bytes=40 * 1024 * 1024
        ),
        cost_estimate=pl.CostEstimate(
            flops=4_000_000_000, bytes_accessed=6_000_000, transcendentals=30_000
        ),
    )(*args)


def solution(mesh, ny=4, nc=2, cap=4):
    nx = mesh.shape["head"]
    nz = mesh.shape["bank"] // (ny * nc)
    return jax.shard_map(
        functools.partial(on_device, (nx, ny, nz, nc, cap)),
        mesh=mesh,
        in_specs=(
            P("bank", None),
            P("bank", None),
            P("bank", None),
            P("bank", None),
            P("bank", None),
            P(),
            P("bank", None),
            P(None, "head"),
            P("head"),
            P("head", None),
        ),
        out_specs=(P(("bank", "head"), None), P("head", None)),
        check_vma=False,
    )
```

```python
import functools
import math

import jax
import jax.numpy as jnp
from jax import lax
from jax.experimental import pallas as pl
from jax.experimental.pallas import tpu as pltpu
from jax.sharding import PartitionSpec as P

MESH = pl.DeviceIdType.MESH
F32 = jnp.float32
BF16 = jnp.bfloat16
I32 = jnp.int32
NEG = 32
BLOCK_ROWS = 128
QH = 8
PAIRS = QH * NEG
K0 = math.sqrt(2.0 / math.pi)
K1 = 0.044715


def iota(shape, axis):
    return lax.broadcasted_iota(I32, shape, axis)


def dot(a, b, ca=1, cb=0):
    return lax.dot_general(a, b, (((ca,), (cb,)), ((), ())), preferred_element_type=F32)


def fold(rows):
    w = rows.shape[1] // 2
    return jnp.concatenate([rows[:, :w], rows[:, w:]], axis=0)


def unfold(rows):
    return jnp.concatenate([rows[:QH], rows[QH:]], axis=1)


def kernel(
    dims,
    in_hbm, pos_hbm, nb_hbm, nr_hbm, mg_hbm, home_hbm, bank_hbm, up_hbm, bias_hbm, down_hbm,
    gi_ref, gd_ref,
    in_ref, pos_ref, nb_ref, nr_ref, mg_ref, home_ref, bank_ref, up_ref, bias_ref, down_ref,
    meta_all, e_all, ps_all, h_two, ht_send, ht_all, f_all, gd_all,
    xs, xr, xs2, xr2, xg, in_l, pos_l, dgelu,
    pm_sc, near_sc, q_sc, m_sc,
    g_own, g_send, gc_recv, gy_send, gy_recv, gz_send, gz_recv,
    r_own, r_send, rc_recv, ry_send, ry_recv, rz_send, rz_recv,
    p_sc, pz_recv,
    lsem, xsem, zsem, ysem, csem,
):
    nx, ny, nz, nc, cap = dims
    per = min(4, nz)
    chunks = nz // per
    rings = ny * per
    block = nc * rings
    slots = cap * block
    b = lax.axis_index("bank")
    x = lax.axis_index("head")
    c = lax.rem(b, nc)
    z = lax.rem(b // nc, nz)
    y = b // (nc * nz)
    oc = 1 - c
    width = in_ref.shape[1]
    half = width // 2
    units = up_ref.shape[1]
    rows_own = bank_ref.shape[0]
    homes = home_ref.shape[1]
    gd_pieces = units // ny // 16
    offs = [(s + 1) // 2 if s % 2 else -(s // 2) for s in range(nz)]

    def bid(yy, zz, cc):
        return (yy * nz + zz) * nc + cc

    def zat(off):
        return lax.rem(z + (off + nz), nz)

    def xdev(d):
        return (b, lax.rem(x + d, nx))

    def xcdev(d):
        return (bid(y, z, oc), lax.rem(x + d, nx))

    def zdev(off):
        return (bid(y, zat(off), c), x)

    def ydev(d):
        return (bid(lax.rem(y + d, ny), z, c), x)

    cdev = xcdev(0)
    unsent = []

    def copy(src, dst, sems, i, dev):
        return pltpu.make_async_remote_copy(
            src_ref=src, dst_ref=dst, send_sem=sems.at[0, i], recv_sem=sems.at[1, i],
            device_id=dev, device_id_type=MESH,
        )

    def start(cp, when=None):
        if when is None:
            cp.start()
        else:
            pl.when(when)(cp.start)
        unsent.append((cp, when))

    def zcopy(k, s, off, src, dst):
        return copy(src, dst, zsem, k * nz + s, zdev(off))

    def ycopy(k, d, src, dst):
        return copy(src, dst, ysem, k * ny + d, ydev(d))

    def ccopy(k, src, dst):
        return copy(src, dst, csem, k, cdev)

    def xcopy(k, d, src, dst):
        return copy(src, dst, xsem, k * nx + d, xdev(d))

    pairs = [
        (in_hbm, in_ref), (up_hbm, up_ref), (bias_hbm, bias_ref), (down_hbm, down_ref),
        (nb_hbm, nb_ref), (nr_hbm, nr_ref), (mg_hbm, mg_ref), (home_hbm, home_ref),
        (pos_hbm, pos_ref), (bank_hbm, bank_ref),
    ]
    loads = [pltpu.make_async_copy(src, dst, lsem.at[i]) for i, (src, dst) in enumerate(pairs)]
    for cp in loads:
        cp.start()

    barrier = pltpu.get_barrier_semaphore()
    greet = [xcdev(d) for d in range(nx)] + [xdev(d) for d in range(1, nx)]
    greet += [ydev(d) for d in range(1, ny)] + []
    greet = [zdev(o) for o in offs[:0:-1]] + greet
    for dev in greet:
        pl.semaphore_signal(barrier, inc=1, device_id=dev, device_id_type=MESH)

    for cp in loads[:4]:
        cp.wait()
    queries = in_ref[...]
    pre = dot(queries, up_ref[...]) + bias_ref[...].reshape(1, units)
    t = jnp.tanh(K0 * (pre + K1 * (pre * pre * pre)))
    hid = (0.5 * pre * (1.0 + t)).astype(BF16)
    h_two[0] = hid
    partial = dot(hid, down_ref[...])
    for i in range(nx):
        xs[i] = fold(partial[QH * i:QH * (i + 1)]).astype(BF16)

    for cp in loads[4:8]:
        cp.wait()
    mine8 = pl.ds(pl.multiple_of(x * QH, QH), QH)
    lanes = 128 // NEG

    def row_of(rows, i):
        return jnp.concatenate([rows[lanes * i + k:lanes * i + k + 1] for k in range(lanes)], axis=1)

    home = home_ref[...]
    part = iota((8, homes), 0)
    home8 = jnp.broadcast_to(home, (8, homes))
    table = jnp.where(part == 0, home8 >> 1, jnp.where(part == 1, home8 & 1, 0))
    table = table.astype(F32).astype(BF16)
    nb8, nr8, mg8 = nb_ref[mine8, :], nr_ref[mine8, :], mg_ref[mine8, :]
    for i in range(PAIRS // 128):
        hot = jnp.where(iota((homes, 128), 0) == row_of(nb8, i), 1.0, 0.0).astype(BF16)
        found = dot(table, hot)
        place = 2.0 * found[0:1] + found[1:2]
        ids = place * float(BLOCK_ROWS) + row_of(nr8, i).astype(F32)
        meta_all[0, 0, :, pl.ds(128 * i, 128)] = ids
        meta_all[0, 0, :, pl.ds(PAIRS + 128 * i, 128)] = row_of(mg8, i)

    pl.semaphore_wait(barrier, len(greet))

    far_first = list(range(nz - 1, 0, -1))

    def zgather(k, s, ref):
        return zcopy(k, s, -offs[s], ref.at[0, pl.ds(0, 1)], ref.at[s // per, pl.ds(s % per, 1)])

    for d in range(1, nx):
        start(xcopy(0, d, xs.at[lax.rem(x + d, nx)], xr.at[d]))
    for s in far_first:
        start(zgather(0, s, meta_all))
    start(ccopy(0, h_two.at[0], h_two.at[1]))
    dgelu[...] = 0.5 * (1.0 + t) + 0.5 * pre * (1.0 - t * t) * (K0 * (1.0 + 3.0 * K1 * (pre * pre)))
    inf = queries.astype(F32)
    loads[8].wait()
    posf = pos_ref[...].astype(F32)
    for i in range(nx):
        in_l[i] = fold(inf[QH * i:QH * (i + 1)])
        pos_l[i] = fold(posf[QH * i:QH * (i + 1)])

    total = xs[x].astype(F32)
    for d in range(1, nx):
        xcopy(0, d, xs.at[0], xr.at[d]).wait_recv()
        total = total + xr[d].astype(F32)
    emb = (in_l[x] + total).astype(BF16)
    e_all[0, 0] = emb
    s16 = jnp.sum(emb.astype(F32) * pos_l[x], axis=1, keepdims=True)
    s8 = s16[:QH] + s16[QH:]
    diag = iota((QH, 128), 0) == iota((QH, 128), 1)
    ps_all[0, 0] = jnp.sum(jnp.where(diag, s8, 0.0), axis=0, keepdims=True)
    for s in far_first:
        start(zgather(1, s, e_all))
        start(zgather(2, s, ps_all))

    def near_ring(ref, k, d=0):
        return ref.at[k, pl.ds(d * per, per)]

    def emb_z(k):
        for s in range(max(1, k * per), (k + 1) * per):
            zgather(1, s, e_all).wait_recv()
            zgather(2, s, ps_all).wait_recv()
        for d in range(1, ny):
            start(ycopy(2 + k, d, near_ring(e_all, k), near_ring(e_all, k, ny - d)))
            start(ycopy(6 + k, d, near_ring(ps_all, k), near_ring(ps_all, k, ny - d)))

    def emb_y(k):
        for d in range(1, ny):
            ycopy(2 + k, d, near_ring(e_all, k), near_ring(e_all, k, ny - d)).wait_recv()
            ycopy(6 + k, d, near_ring(ps_all, k), near_ring(ps_all, k, ny - d)).wait_recv()
        start(emb_core(2 + k, e_all, k))
        start(emb_core(6 + k, ps_all, k))

    def emb_core(i, ref, k):
        return ccopy(i, ref.at[k, pl.ds(0, rings)], ref.at[k, pl.ds(rings, rings)])

    ccopy(0, h_two.at[0], h_two.at[1]).wait_recv()
    turned = jnp.concatenate([h_two[0].astype(F32), h_two[1].astype(F32)], axis=0).T
    ht_send[...] = turned.astype(BF16).reshape(ht_send.shape)
    for d in range(1, ny):
        start(ycopy(0, d, ht_send.at[lax.rem(y + d, ny)], ht_all.at[ny - d]))
    ht_all[0] = ht_send[y]

    for s in range(1, nz):
        zgather(0, s, meta_all).wait_recv()

    def meta_y(d):
        return ycopy(
            1, d, meta_all.at[:, pl.ds(0, per)], meta_all.at[:, pl.ds((ny - d) * per, per)]
        )

    for d in range(1, ny):
        start(meta_y(d))
    for d in range(1, ny):
        meta_y(d).wait_recv()
    meta_c = ccopy(1, meta_all.at[:, pl.ds(0, rings)], meta_all.at[:, pl.ds(rings, rings)])
    start(meta_c)
    emb_z(0)
    meta_c.wait_recv()
    loads[9].wait()

    tri = jnp.where(iota((PAIRS, PAIRS), 0) <= iota((PAIRS, PAIRS), 1), 1.0, 0.0).astype(BF16)
    q_lane = (iota((block, PAIRS), 1) // NEG + 1).astype(F32)
    def find(k):
        ids = meta_all[k, :, 0, pl.ds(0, PAIRS)].astype(I32)
        margins = meta_all[k, :, 0, pl.ds(PAIRS, PAIRS)]
        owner = ids // rows_own
        local = (ids - owner * rows_own).astype(F32)
        mine = owner == b
        prefix = dot(jnp.where(mine, 1.0, 0.0).astype(BF16), tri)
        pm = jnp.where(mine, prefix, 0.0)
        pm_sc[k] = pm
        rows, qs, ms = [], [], []
        for r in range(cap):
            sel = pm == float(r + 1)
            rows.append(jnp.sum(jnp.where(sel, local, 0.0), axis=1, keepdims=True))
            qs.append(jnp.sum(jnp.where(sel, q_lane, 0.0), axis=1, keepdims=True))
            ms.append(jnp.sum(jnp.where(sel, margins, 0.0), axis=1, keepdims=True))
        rows, qs = jnp.concatenate(rows, axis=0), jnp.concatenate(qs, axis=0)
        q_sc[k] = qs
        m_sc[k] = jnp.concatenate(ms, axis=0)
        row_i = jnp.where(qs > 0.5, rows, -1.0).astype(I32)
        hot_row = jnp.where(iota((slots, rows_own), 1) == row_i, 1.0, 0.0).astype(BF16)
        near_sc[k] = dot(hot_row, bank_ref[...]).astype(BF16)

    ind = jnp.where(iota((PAIRS, 128), 0) // NEG == iota((PAIRS, 128), 1), 1.0, 0.0).astype(BF16)

    def score(k):
        emb_core(2 + k, e_all, k).wait_recv()
        emb_core(6 + k, ps_all, k).wait_recv()
        qs = q_sc[k]
        q_i = qs.astype(I32) - 1
        ps_rep = jnp.concatenate([ps_all[k, :, 0, :]] * cap, axis=0)
        ps = jnp.sum(jnp.where(iota((slots, 128), 1) == q_i, ps_rep, 0.0), axis=1, keepdims=True)
        offsets = (ps - m_sc[k]).astype(BF16).astype(F32)
        group_i = lax.rem(iota((slots, 1), 0), block)
        target = jnp.where(qs > 0.5, group_i * 16 + q_i, -100)
        target = jnp.concatenate([target, target + QH], axis=0)
        hot_q = jnp.where(iota((2 * slots, block * 16), 1) == target, 1.0, 0.0).astype(BF16)
        embs = dot(hot_q, e_all[k].reshape(block * 16, half))
        near = near_sc[k].astype(F32)
        found = jnp.sum(
            embs[:slots] * near[:, :half] + embs[slots:] * near[:, half:], axis=1, keepdims=True
        )
        residual = offsets - found
        weighted = (residual * near).astype(BF16)
        weighted = jnp.concatenate([weighted[:, :half], weighted[:, half:]], axis=0)
        summed = dot(hot_q, weighted, 0, 0).reshape(block, 16, half)
        rounded = residual.astype(BF16).astype(F32)
        pm = pm_sc[k]
        per_pair = jnp.zeros((block, PAIRS), F32)
        for r in range(cap):
            per_pair = per_pair + jnp.where(
                pm == float(r + 1), rounded[r * block:(r + 1) * block], 0.0
            )
        rsum = dot(per_pair.astype(BF16), ind)
        g_send[k] = summed[rings:].astype(BF16)
        r_send[k, :, 0, :] = rsum[rings:]
        start(ccopy(10 + k, g_send.at[k], gc_recv.at[k]))
        start(ccopy(14 + k, r_send.at[k], rc_recv.at[k]))
        g_own[k] = summed[:rings]
        r_own[k, :, 0, :] = rsum[:rings]

    def sum_core(k):
        ccopy(10 + k, g_send.at[k], gc_recv.at[k]).wait_recv()
        ccopy(14 + k, r_send.at[k], rc_recv.at[k]).wait_recv()
        for d in list(range(1, ny)) + [0]:
            at = pl.ds(d * per, per)
            g_sum = g_own[k, at] + gc_recv[k, at].astype(F32)
            r_sum = r_own[k, at] + rc_recv[k, at]
            if d:
                gy_send[k, d] = g_sum.astype(BF16)
                ry_send[k, d] = r_sum
                start(ycopy(10 + k, d, gy_send.at[k, d], gy_recv.at[k, d]))
                start(ycopy(14 + k, d, ry_send.at[k, d], ry_recv.at[k, d]))
            else:
                g_own[k, at] = g_sum
                r_own[k, at] = r_sum

    def sum_y(k):
        g_sum = g_own[k, pl.ds(0, per)]
        r_sum = r_own[k, pl.ds(0, per)]
        for d in range(1, ny):
            ycopy(10 + k, d, gy_send.at[k, d], gy_recv.at[k, d]).wait_recv()
            ycopy(14 + k, d, ry_send.at[k, d], ry_recv.at[k, d]).wait_recv()
            g_sum = g_sum + gy_recv[k, d].astype(F32)
            r_sum = r_sum + ry_recv[k, d]
        gz_send[k] = g_sum.astype(BF16)
        rz_send[k] = r_sum
        if k == 0:
            g_own[0, 0] = g_sum[0]
        for s in range((k + 1) * per - 1, max(1, k * per) - 1, -1):
            start(zcopy(3, s, offs[s], gz_send.at[k, s % per], gz_recv.at[s]))
            start(zcopy(4, s, offs[s], rz_send.at[k, s % per], rz_recv.at[s]))

    find(0)
    stages = [emb_z, find, emb_y, score, sum_core, sum_y]
    lag = [0, 0, 1, 2, 3, 4]
    for step in range(1, chunks + max(lag)):
        for stage, late in zip(stages, lag):
            if 0 <= step - late < chunks:
                stage(step - late)

    wsum = g_own[0, 0]
    rsum = rz_send[0, 0]
    for s in range(1, nz):
        zcopy(3, s, offs[s], gz_send.at[0, 0], gz_recv.at[s]).wait_recv()
        zcopy(4, s, offs[s], rz_send.at[0, 0], rz_recv.at[s]).wait_recv()
        wsum = wsum + gz_recv[s].astype(F32)
        rsum = rsum + rz_recv[s]
    lane_q = iota((16, 128), 1) == lax.rem(iota((16, 128), 0), QH)
    rcol = jnp.sum(jnp.where(lane_q, rsum, 0.0), axis=1, keepdims=True)
    gradient = 2.0 * pos_l[x] * rcol - 2.0 * wsum
    xg[0, x] = gradient.astype(BF16)
    for d in range(1, nx):
        start(xcopy(1, d, xg.at[0, x], xg.at[0, x]))
    for d in range(nx):
        start(copy(xg.at[0, x], xg.at[1, x], xsem, 3 * nx + d, xcdev(d)))
    for d in range(nx):
        src = lax.rem(x + nx - d, nx)
        if d:
            xcopy(1, d, xg.at[0, x], xg.at[0, src]).wait_recv()
        copy(xg.at[0, x], xg.at[1, src], xsem, 3 * nx + d, xcdev(d)).wait_recv()

    def halves(cr):
        pieces = [xg[cr, i].astype(F32) for i in range(nx)]
        top = jnp.concatenate([p[:QH] for p in pieces], axis=0)
        low = jnp.concatenate([p[QH:] for p in pieces], axis=0)
        f_all[0, cr] = jnp.where(c == 0, top, low).astype(BF16)
        return top, low

    top, low = halves(0)
    halves(1)
    for d in range(1, ny):
        start(ycopy(18, d, f_all.at[0], f_all.at[ny - d]))

    down_sum = dot(ht_all[0], f_all[0].reshape(nc * nx * QH, half))
    for d in range(1, ny):
        ycopy(0, d, ht_send.at[0], ht_all.at[ny - d]).wait_recv()
        ycopy(18, d, f_all.at[0], f_all.at[ny - d]).wait_recv()
        down_sum = down_sum + dot(ht_all[ny - d], f_all[ny - d].reshape(nc * nx * QH, half))
    p_sc[...] = down_sum.astype(BF16).reshape(gd_pieces, 16, half)
    for s in far_first:
        zz = zat(offs[s])
        piece = p_sc.at[jnp.minimum(zz, gd_pieces - 1)]
        start(zcopy(5, s, offs[s], piece, pz_recv.at[s]), zz < gd_pieces)

    grad_all = jnp.concatenate([top, low], axis=1).astype(BF16)
    hidden_grad = dot(grad_all, down_ref[...], 1, 1)
    pre_grad = (hidden_grad * dgelu[...]).astype(BF16)
    carried = dot(pre_grad, up_ref[...], 1, 1)
    for i in range(nx):
        xs2[i] = fold(carried[QH * i:QH * (i + 1)]).astype(BF16)
    for d in range(1, nx):
        start(xcopy(2, d, xs2.at[lax.rem(x + d, nx)], xr2.at[d]))

    busy = z < gd_pieces
    scale = 1.0 / math.sqrt(nx * QH * ny * nz * nc)

    @pl.when(busy)
    def _():
        acc = p_sc[jnp.minimum(z, gd_pieces - 1)].astype(F32)
        for s in range(1, nz):
            zcopy(5, s, offs[s], p_sc.at[0], pz_recv.at[s]).wait_recv()
            acc = acc + pz_recv[s].astype(F32)
        gd_all[0, 0] = (acc * scale).astype(BF16)

    def zlast(s):
        return zgather(6, s, gd_all)

    for s in far_first:
        start(zlast(s), busy)

    carry = xs2[x].astype(F32) + gradient
    for d in range(1, nx):
        xcopy(2, d, xs2.at[0], xr2.at[d]).wait_recv()
        carry = carry + xr2[d].astype(F32)
    gi_ref[...] = unfold(carry).astype(BF16)

    def last_z(k):
        for s in range(max(1, k * per), (k + 1) * per):
            pl.when(zat(offs[s]) < gd_pieces)(zlast(s).wait_recv)
        for d in range(1, ny):
            start(ycopy(19 + k, d, near_ring(gd_all, k), near_ring(gd_all, k, ny - d)))

    def last_y(k):
        for d in range(1, ny):
            ycopy(19 + k, d, near_ring(gd_all, k), near_ring(gd_all, k, ny - d)).wait_recv()
        start(emb_core(18 + k, gd_all, k))
        put(k, 0)

    def put(k, cr):
        at = c if cr == 0 else oc
        for s in range(per):
            zz = zat(offs[k * per + s])

            @pl.when(zz < gd_pieces)
            def _():
                for d in range(ny):
                    yy = lax.rem(y + d, ny)
                    row = pl.multiple_of((yy * gd_pieces + zz) * 16, 16)
                    col = pl.multiple_of(at * half, 128)
                    gd_ref[pl.ds(row, 16), pl.ds(col, half)] = gd_all[k, cr * rings + d * per + s]

    def last_core(k):
        emb_core(18 + k, gd_all, k).wait_recv()
        put(k, 1)

    stages = [last_z, last_y, last_core]
    for step in range(chunks + len(stages) - 1):
        for late, stage in enumerate(stages):
            if 0 <= step - late < chunks:
                stage(step - late)

    for cp, when in unsent:
        if when is None:
            cp.wait_send()
        else:
            pl.when(when)(cp.wait_send)


def on_device(
    dims, inputs, positives, margins, neg_block, neg_row, block_home, bank, up_weight, up_bias,
    down_weight,
):
    nx, ny, nz, nc, cap = dims
    width = inputs.shape[1]
    half = width // 2
    units = up_weight.shape[1]
    queries = inputs.shape[0]
    per = min(4, nz)
    chunks = nz // per
    rings = ny * per
    block = nc * rings
    slots = cap * block
    gd_pieces = units // ny // 16
    V = pltpu.VMEM
    args = (
        inputs, positives, neg_block, neg_row, margins, block_home.reshape(1, -1), bank,
        up_weight, up_bias, down_weight,
    )
    scratch = [V(a.shape, a.dtype) for a in args] + [
        V((chunks, block, 1, 2 * PAIRS), F32),
        V((chunks, block, 16, half), BF16),
        V((chunks, block, 1, 128), F32),
        V((nc, queries, units), BF16),
        V((ny, units // ny, nc * queries), BF16),
        V((ny, units // ny, nc * queries), BF16),
        V((ny, nc, queries, half), BF16),
        V((chunks, block, 16, half), BF16),
        V((nx, 16, half), BF16),
        V((nx, 16, half), BF16),
        V((nx, 16, half), BF16),
        V((nx, 16, half), BF16),
        V((nc, nx, 16, half), BF16),
        V((nx, 16, half), F32),
        V((nx, 16, half), F32),
        V((queries, units), F32),
        V((chunks, block, PAIRS), F32),
        V((chunks, slots, width), BF16),
        V((chunks, slots, 1), F32),
        V((chunks, slots, 1), F32),
        V((chunks, rings, 16, half), F32),
        V((chunks, rings, 16, half), BF16),
        V((chunks, rings, 16, half), BF16),
        V((chunks, ny, per, 16, half), BF16),
        V((chunks, ny, per, 16, half), BF16),
        V((chunks, per, 16, half), BF16),
        V((nz, 16, half), BF16),
        V((chunks, rings, 1, 128), F32),
        V((chunks, rings, 1, 128), F32),
        V((chunks, rings, 1, 128), F32),
        V((chunks, ny, per, 1, 128), F32),
        V((chunks, ny, per, 1, 128), F32),
        V((chunks, per, 1, 128), F32),
        V((nz, 1, 128), F32),
        V((gd_pieces, 16, half), BF16),
        V((nz, 16, half), BF16),
        pltpu.SemaphoreType.DMA((len(args),)),
        pltpu.SemaphoreType.DMA((2, 4 * nx)),
        pltpu.SemaphoreType.DMA((2, 7 * nz)),
        pltpu.SemaphoreType.DMA((2, 23 * ny)),
        pltpu.SemaphoreType.DMA((2, 22)),
    ]
    vmem = pl.BlockSpec(memory_space=pltpu.VMEM)
    return pl.pallas_call(
        functools.partial(kernel, dims),
        out_shape=(
            jax.ShapeDtypeStruct((QH, width), BF16),
            jax.ShapeDtypeStruct((units, width), BF16),
        ),
        in_specs=[pl.BlockSpec(memory_space=pltpu.HBM)] * len(args),
        out_specs=(vmem, vmem),
        scratch_shapes=scratch,
        compiler_params=pltpu.CompilerParams(
            collective_id=0, has_side_effects=True, vmem_limit_bytes=60 * 1024 * 1024
        ),
        cost_estimate=pl.CostEstimate(
            flops=4_000_000_000, bytes_accessed=6_000_000, transcendentals=30_000
        ),
    )(*args)


def solution(mesh, ny=4, nc=2, cap=4):
    nx = mesh.shape["head"]
    nz = mesh.shape["bank"] // (ny * nc)
    return jax.shard_map(
        functools.partial(on_device, (nx, ny, nz, nc, cap)),
        mesh=mesh,
        in_specs=(
            P("bank", None),
            P("bank", None),
            P("bank", None),
            P("bank", None),
            P("bank", None),
            P(),
            P("bank", None),
            P(None, "head"),
            P("head"),
            P("head", None),
        ),
        out_specs=(P(("bank", "head"), None), P("head", None)),
        check_vma=False,
    )
```

```python
import functools
import math

import jax
import jax.numpy as jnp
from jax import lax
from jax.experimental import pallas as pl
from jax.experimental.pallas import tpu as pltpu
from jax.sharding import PartitionSpec as P

MESH = pl.DeviceIdType.MESH
F32 = jnp.float32
BF16 = jnp.bfloat16
I32 = jnp.int32
NEG = 32
BLOCK_ROWS = 128
QH = 8
PAIRS = QH * NEG
K0 = math.sqrt(2.0 / math.pi)
K1 = 0.044715


def iota(shape, axis):
    return lax.broadcasted_iota(I32, shape, axis)


def dot(a, b, ca=1, cb=0):
    return lax.dot_general(a, b, (((ca,), (cb,)), ((), ())), preferred_element_type=F32)


def fold(rows):
    w = rows.shape[1] // 2
    return jnp.concatenate([rows[:, :w], rows[:, w:]], axis=0)


def unfold(rows):
    return jnp.concatenate([rows[:QH], rows[QH:]], axis=1)


def kernel(
    dims,
    in_hbm, pos_hbm, nb_hbm, nr_hbm, mg_hbm, home_hbm, bank_hbm, up_hbm, bias_hbm, down_hbm,
    gi_ref, gd_ref,
    in_ref, pos_ref, nb_ref, nr_ref, mg_ref, home_ref, bank_ref, up_ref, bias_ref, down_ref,
    meta_all, e_all, ps_all, h_two, ht_send, ht_all, f_all, gd_all,
    xs, xr, xs2, xr2, xg, in_l, pos_l, dgelu,
    pm_sc, near_sc, q_sc, m_sc,
    g_own, g_send, gc_recv, gy_send, gy_recv, gz_send, gz_recv,
    r_own, r_send, rc_recv, ry_send, ry_recv, rz_send, rz_recv,
    p_sc, pz_recv,
    lsem, xsem, zsem, ysem, csem,
):
    nx, ny, nz, nc, cap = dims
    per = min(4, nz)
    chunks = nz // per
    rings = ny * per
    block = nc * rings
    slots = cap * block
    b = lax.axis_index("bank")
    x = lax.axis_index("head")
    c = lax.rem(b, nc)
    z = lax.rem(b // nc, nz)
    y = b // (nc * nz)
    oc = 1 - c
    width = in_ref.shape[1]
    half = width // 2
    units = up_ref.shape[1]
    rows_own = bank_ref.shape[0]
    homes = home_ref.shape[1]
    gd_pieces = units // ny // 16
    offs = [(s + 1) // 2 if s % 2 else -(s // 2) for s in range(nz)]

    def bid(yy, zz, cc):
        return (yy * nz + zz) * nc + cc

    def zat(off):
        return lax.rem(z + (off + nz), nz)

    def xdev(d):
        return (b, lax.rem(x + d, nx))

    def xcdev(d):
        return (bid(y, z, oc), lax.rem(x + d, nx))

    def zdev(off):
        return (bid(y, zat(off), c), x)

    def ydev(d):
        return (bid(lax.rem(y + d, ny), z, c), x)

    def piece_of(zz):
        return zz * gd_pieces // nz

    def owns(zz):
        return piece_of(zz + 1) > piece_of(zz)

    cdev = xcdev(0)
    unsent = []

    def copy(src, dst, sems, i, dev):
        return pltpu.make_async_remote_copy(
            src_ref=src, dst_ref=dst, send_sem=sems.at[0, i], recv_sem=sems.at[1, i],
            device_id=dev, device_id_type=MESH,
        )

    def start(cp, when=None):
        if when is None:
            cp.start()
        else:
            pl.when(when)(cp.start)
        unsent.append((cp, when))

    def zcopy(k, s, off, src, dst):
        return copy(src, dst, zsem, k * nz + s, zdev(off))

    def ycopy(k, d, src, dst):
        return copy(src, dst, ysem, k * ny + d, ydev(d))

    def ccopy(k, src, dst):
        return copy(src, dst, csem, k, cdev)

    def xcopy(k, d, src, dst):
        return copy(src, dst, xsem, k * nx + d, xdev(d))

    pairs = [
        (in_hbm, in_ref), (up_hbm, up_ref), (bias_hbm, bias_ref), (down_hbm, down_ref),
        (nb_hbm, nb_ref), (nr_hbm, nr_ref), (mg_hbm, mg_ref), (home_hbm, home_ref),
        (pos_hbm, pos_ref), (bank_hbm, bank_ref),
    ]
    loads = [pltpu.make_async_copy(src, dst, lsem.at[i]) for i, (src, dst) in enumerate(pairs)]
    for cp in loads:
        cp.start()

    barrier = pltpu.get_barrier_semaphore()
    greet = [xcdev(d) for d in range(nx)] + [xdev(d) for d in range(1, nx)]
    greet += [ydev(d) for d in range(1, ny)] + []
    greet = [zdev(o) for o in offs[:0:-1]] + greet
    for dev in greet:
        pl.semaphore_signal(barrier, inc=1, device_id=dev, device_id_type=MESH)

    for cp in loads[:4]:
        cp.wait()
    queries = in_ref[...]
    pre = dot(queries, up_ref[...]) + bias_ref[...].reshape(1, units)
    t = jnp.tanh(K0 * (pre + K1 * (pre * pre * pre)))
    hid = (0.5 * pre * (1.0 + t)).astype(BF16)
    h_two[0] = hid
    partial = dot(hid, down_ref[...])
    for i in range(nx):
        xs[i] = fold(partial[QH * i:QH * (i + 1)]).astype(BF16)

    for cp in loads[4:8]:
        cp.wait()
    mine8 = pl.ds(pl.multiple_of(x * QH, QH), QH)
    lanes = 128 // NEG

    def row_of(rows, i):
        return jnp.concatenate([rows[lanes * i + k:lanes * i + k + 1] for k in range(lanes)], axis=1)

    home = home_ref[...]
    part = iota((8, homes), 0)
    home8 = jnp.broadcast_to(home, (8, homes))
    table = jnp.where(part == 0, home8 >> 1, jnp.where(part == 1, home8 & 1, 0))
    table = table.astype(F32).astype(BF16)
    nb8, nr8, mg8 = nb_ref[mine8, :], nr_ref[mine8, :], mg_ref[mine8, :]
    for i in range(PAIRS // 128):
        hot = jnp.where(iota((homes, 128), 0) == row_of(nb8, i), 1.0, 0.0).astype(BF16)
        found = dot(table, hot)
        place = 2.0 * found[0:1] + found[1:2]
        ids = place * float(BLOCK_ROWS) + row_of(nr8, i).astype(F32)
        meta_all[0, 0, :, pl.ds(128 * i, 128)] = ids
        meta_all[0, 0, :, pl.ds(PAIRS + 128 * i, 128)] = row_of(mg8, i)

    pl.semaphore_wait(barrier, len(greet))

    far_first = list(range(nz - 1, 0, -1))

    def zgather(k, s, ref):
        return zcopy(k, s, -offs[s], ref.at[0, pl.ds(0, 1)], ref.at[s // per, pl.ds(s % per, 1)])

    for d in range(1, nx):
        start(xcopy(0, d, xs.at[lax.rem(x + d, nx)], xr.at[d]))
    for s in far_first:
        start(zgather(0, s, meta_all))
    start(ccopy(0, h_two.at[0], h_two.at[1]))
    dgelu[...] = 0.5 * (1.0 + t) + 0.5 * pre * (1.0 - t * t) * (K0 * (1.0 + 3.0 * K1 * (pre * pre)))
    inf = queries.astype(F32)
    loads[8].wait()
    posf = pos_ref[...].astype(F32)
    for i in range(nx):
        in_l[i] = fold(inf[QH * i:QH * (i + 1)])
        pos_l[i] = fold(posf[QH * i:QH * (i + 1)])

    total = xs[x].astype(F32)
    for d in range(1, nx):
        xcopy(0, d, xs.at[0], xr.at[d]).wait_recv()
        total = total + xr[d].astype(F32)
    emb = (in_l[x] + total).astype(BF16)
    e_all[0, 0] = emb
    s16 = jnp.sum(emb.astype(F32) * pos_l[x], axis=1, keepdims=True)
    s8 = s16[:QH] + s16[QH:]
    diag = iota((QH, 128), 0) == iota((QH, 128), 1)
    ps_all[0, 0] = jnp.sum(jnp.where(diag, s8, 0.0), axis=0, keepdims=True)
    for s in range(1, nz):
        start(zgather(1, s, e_all))
        start(zgather(2, s, ps_all))

    def near_ring(ref, k, d=0):
        return ref.at[k, pl.ds(d * per, per)]

    def emb_z(k):
        for s in range(max(1, k * per), (k + 1) * per):
            zgather(1, s, e_all).wait_recv()
            zgather(2, s, ps_all).wait_recv()
        for d in range(1, ny):
            start(ycopy(2 + k, d, near_ring(e_all, k), near_ring(e_all, k, ny - d)))
            start(ycopy(6 + k, d, near_ring(ps_all, k), near_ring(ps_all, k, ny - d)))

    def emb_y(k):
        for d in range(1, ny):
            ycopy(2 + k, d, near_ring(e_all, k), near_ring(e_all, k, ny - d)).wait_recv()
            ycopy(6 + k, d, near_ring(ps_all, k), near_ring(ps_all, k, ny - d)).wait_recv()
        start(emb_core(2 + k, e_all, k))
        start(emb_core(6 + k, ps_all, k))

    def emb_core(i, ref, k):
        return ccopy(i, ref.at[k, pl.ds(0, rings)], ref.at[k, pl.ds(rings, rings)])

    ccopy(0, h_two.at[0], h_two.at[1]).wait_recv()
    turned = jnp.concatenate([h_two[0].astype(F32), h_two[1].astype(F32)], axis=0).T
    ht_send[...] = turned.astype(BF16).reshape(ht_send.shape)
    for d in range(1, ny):
        start(ycopy(0, d, ht_send.at[lax.rem(y + d, ny)], ht_all.at[ny - d]))
    ht_all[0] = ht_send[y]

    for s in range(1, nz):
        zgather(0, s, meta_all).wait_recv()

    def meta_y(d):
        return ycopy(
            1, d, meta_all.at[:, pl.ds(0, per)], meta_all.at[:, pl.ds((ny - d) * per, per)]
        )

    for d in range(1, ny):
        start(meta_y(d))
    for d in range(1, ny):
        meta_y(d).wait_recv()
    meta_c = ccopy(1, meta_all.at[:, pl.ds(0, rings)], meta_all.at[:, pl.ds(rings, rings)])
    start(meta_c)
    emb_z(0)
    meta_c.wait_recv()
    loads[9].wait()

    tri = jnp.where(iota((PAIRS, PAIRS), 0) <= iota((PAIRS, PAIRS), 1), 1.0, 0.0).astype(BF16)
    q_lane = (iota((block, PAIRS), 1) // NEG + 1).astype(F32)
    def find(k):
        ids = meta_all[k, :, 0, pl.ds(0, PAIRS)].astype(I32)
        margins = meta_all[k, :, 0, pl.ds(PAIRS, PAIRS)]
        owner = ids // rows_own
        local = (ids - owner * rows_own).astype(F32)
        mine = owner == b
        prefix = dot(jnp.where(mine, 1.0, 0.0).astype(BF16), tri)
        pm = jnp.where(mine, prefix, 0.0)
        pm_sc[k] = pm
        rows, qs, ms = [], [], []
        for r in range(cap):
            sel = pm == float(r + 1)
            rows.append(jnp.sum(jnp.where(sel, local, 0.0), axis=1, keepdims=True))
            qs.append(jnp.sum(jnp.where(sel, q_lane, 0.0), axis=1, keepdims=True))
            ms.append(jnp.sum(jnp.where(sel, margins, 0.0), axis=1, keepdims=True))
        rows, qs = jnp.concatenate(rows, axis=0), jnp.concatenate(qs, axis=0)
        q_sc[k] = qs
        m_sc[k] = jnp.concatenate(ms, axis=0)
        row_i = jnp.where(qs > 0.5, rows, -1.0).astype(I32)
        hot_row = jnp.where(iota((slots, rows_own), 1) == row_i, 1.0, 0.0).astype(BF16)
        near_sc[k] = dot(hot_row, bank_ref[...]).astype(BF16)

    ind = jnp.where(iota((PAIRS, 128), 0) // NEG == iota((PAIRS, 128), 1), 1.0, 0.0).astype(BF16)

    def score(k):
        emb_core(2 + k, e_all, k).wait_recv()
        emb_core(6 + k, ps_all, k).wait_recv()
        qs = q_sc[k]
        q_i = qs.astype(I32) - 1
        ps_rep = jnp.concatenate([ps_all[k, :, 0, :]] * cap, axis=0)
        ps = jnp.sum(jnp.where(iota((slots, 128), 1) == q_i, ps_rep, 0.0), axis=1, keepdims=True)
        offsets = (ps - m_sc[k]).astype(BF16).astype(F32)
        group_i = lax.rem(iota((slots, 1), 0), block)
        target = jnp.where(qs > 0.5, group_i * 16 + q_i, -100)
        target = jnp.concatenate([target, target + QH], axis=0)
        hot_q = jnp.where(iota((2 * slots, block * 16), 1) == target, 1.0, 0.0).astype(BF16)
        embs = dot(hot_q, e_all[k].reshape(block * 16, half))
        near = near_sc[k].astype(F32)
        found = jnp.sum(
            embs[:slots] * near[:, :half] + embs[slots:] * near[:, half:], axis=1, keepdims=True
        )
        residual = offsets - found
        weighted = (residual * near).astype(BF16)
        weighted = jnp.concatenate([weighted[:, :half], weighted[:, half:]], axis=0)
        summed = dot(hot_q, weighted, 0, 0).reshape(block, 16, half)
        rounded = residual.astype(BF16).astype(F32)
        pm = pm_sc[k]
        per_pair = jnp.zeros((block, PAIRS), F32)
        for r in range(cap):
            per_pair = per_pair + jnp.where(
                pm == float(r + 1), rounded[r * block:(r + 1) * block], 0.0
            )
        rsum = dot(per_pair.astype(BF16), ind)
        g_send[k] = summed[rings:].astype(BF16)
        r_send[k, :, 0, :] = rsum[rings:]
        start(ccopy(10 + k, g_send.at[k], gc_recv.at[k]))
        start(ccopy(14 + k, r_send.at[k], rc_recv.at[k]))
        g_own[k] = summed[:rings]
        r_own[k, :, 0, :] = rsum[:rings]

    def sum_core(k):
        ccopy(10 + k, g_send.at[k], gc_recv.at[k]).wait_recv()
        ccopy(14 + k, r_send.at[k], rc_recv.at[k]).wait_recv()
        for d in list(range(1, ny)) + [0]:
            at = pl.ds(d * per, per)
            g_sum = g_own[k, at] + gc_recv[k, at].astype(F32)
            r_sum = r_own[k, at] + rc_recv[k, at]
            if d:
                gy_send[k, d] = g_sum.astype(BF16)
                ry_send[k, d] = r_sum
                start(ycopy(10 + k, d, gy_send.at[k, d], gy_recv.at[k, d]))
                start(ycopy(14 + k, d, ry_send.at[k, d], ry_recv.at[k, d]))
            else:
                g_own[k, at] = g_sum
                r_own[k, at] = r_sum

    def sum_y(k):
        g_sum = g_own[k, pl.ds(0, per)]
        r_sum = r_own[k, pl.ds(0, per)]
        for d in range(1, ny):
            ycopy(10 + k, d, gy_send.at[k, d], gy_recv.at[k, d]).wait_recv()
            ycopy(14 + k, d, ry_send.at[k, d], ry_recv.at[k, d]).wait_recv()
            g_sum = g_sum + gy_recv[k, d].astype(F32)
            r_sum = r_sum + ry_recv[k, d]
        gz_send[k] = g_sum.astype(BF16)
        rz_send[k] = r_sum
        if k == 0:
            g_own[0, 0] = g_sum[0]
        for s in range((k + 1) * per - 1, max(1, k * per) - 1, -1):
            start(zcopy(3, s, offs[s], gz_send.at[k, s % per], gz_recv.at[s]))
            start(zcopy(4, s, offs[s], rz_send.at[k, s % per], rz_recv.at[s]))

    find(0)
    stages = [emb_z, find, emb_y, score, sum_core, sum_y]
    lag = [0, 0, 1, 2, 3, 4]
    for step in range(1, chunks + max(lag)):
        for stage, late in zip(stages, lag):
            if 0 <= step - late < chunks:
                stage(step - late)

    wsum = g_own[0, 0]
    rsum = rz_send[0, 0]
    for s in range(1, nz):
        zcopy(3, s, offs[s], gz_send.at[0, 0], gz_recv.at[s]).wait_recv()
        zcopy(4, s, offs[s], rz_send.at[0, 0], rz_recv.at[s]).wait_recv()
        wsum = wsum + gz_recv[s].astype(F32)
        rsum = rsum + rz_recv[s]
    lane_q = iota((16, 128), 1) == lax.rem(iota((16, 128), 0), QH)
    rcol = jnp.sum(jnp.where(lane_q, rsum, 0.0), axis=1, keepdims=True)
    gradient = 2.0 * pos_l[x] * rcol - 2.0 * wsum
    xg[0, x] = gradient.astype(BF16)
    for d in range(1, nx):
        start(xcopy(1, d, xg.at[0, x], xg.at[0, x]))
    for d in range(nx):
        start(copy(xg.at[0, x], xg.at[1, x], xsem, 3 * nx + d, xcdev(d)))
    for d in range(nx):
        src = lax.rem(x + nx - d, nx)
        if d:
            xcopy(1, d, xg.at[0, x], xg.at[0, src]).wait_recv()
        copy(xg.at[0, x], xg.at[1, src], xsem, 3 * nx + d, xcdev(d)).wait_recv()

    def halves(cr):
        pieces = [xg[cr, i].astype(F32) for i in range(nx)]
        top = jnp.concatenate([p[:QH] for p in pieces], axis=0)
        low = jnp.concatenate([p[QH:] for p in pieces], axis=0)
        f_all[0, cr] = jnp.where(c == 0, top, low).astype(BF16)
        return top, low

    top, low = halves(0)
    halves(1)
    for d in range(1, ny):
        start(ycopy(18, d, f_all.at[0], f_all.at[ny - d]))

    down_sum = dot(ht_all[0], f_all[0].reshape(nc * nx * QH, half))
    for d in range(1, ny):
        ycopy(0, d, ht_send.at[0], ht_all.at[ny - d]).wait_recv()
        ycopy(18, d, f_all.at[0], f_all.at[ny - d]).wait_recv()
        down_sum = down_sum + dot(ht_all[ny - d], f_all[ny - d].reshape(nc * nx * QH, half))
    p_sc[...] = down_sum.astype(BF16).reshape(gd_pieces, 16, half)
    for s in far_first:
        zz = zat(offs[s])
        start(zcopy(5, s, offs[s], p_sc.at[piece_of(zz)], pz_recv.at[s]), owns(zz))

    grad_all = jnp.concatenate([top, low], axis=1).astype(BF16)
    hidden_grad = dot(grad_all, down_ref[...], 1, 1)
    pre_grad = (hidden_grad * dgelu[...]).astype(BF16)
    carried = dot(pre_grad, up_ref[...], 1, 1)
    for i in range(nx):
        xs2[i] = fold(carried[QH * i:QH * (i + 1)]).astype(BF16)
    for d in range(1, nx):
        start(xcopy(2, d, xs2.at[lax.rem(x + d, nx)], xr2.at[d]))

    busy = owns(z)
    scale = 1.0 / math.sqrt(nx * QH * ny * nz * nc)

    @pl.when(busy)
    def _():
        acc = p_sc[piece_of(z)].astype(F32)
        for s in range(1, nz):
            zcopy(5, s, offs[s], p_sc.at[0], pz_recv.at[s]).wait_recv()
            acc = acc + pz_recv[s].astype(F32)
        gd_all[0, 0] = (acc * scale).astype(BF16)

    def zlast(s):
        return zgather(6, s, gd_all)

    for s in far_first:
        start(zlast(s), busy)

    carry = xs2[x].astype(F32) + gradient
    for d in range(1, nx):
        xcopy(2, d, xs2.at[0], xr2.at[d]).wait_recv()
        carry = carry + xr2[d].astype(F32)
    gi_ref[...] = unfold(carry).astype(BF16)

    def last_z(k):
        for s in range(max(1, k * per), (k + 1) * per):
            pl.when(owns(zat(offs[s])))(zlast(s).wait_recv)
        for d in range(1, ny):
            start(ycopy(19 + k, d, near_ring(gd_all, k), near_ring(gd_all, k, ny - d)))

    def last_y(k):
        for d in range(1, ny):
            ycopy(19 + k, d, near_ring(gd_all, k), near_ring(gd_all, k, ny - d)).wait_recv()
        start(emb_core(18 + k, gd_all, k))
        put(k, 0)

    def put(k, cr):
        at = c if cr == 0 else oc
        for s in range(per):
            zz = zat(offs[k * per + s])

            @pl.when(owns(zz))
            def _():
                for d in range(ny):
                    yy = lax.rem(y + d, ny)
                    row = pl.multiple_of((yy * gd_pieces + piece_of(zz)) * 16, 16)
                    col = pl.multiple_of(at * half, 128)
                    gd_ref[pl.ds(row, 16), pl.ds(col, half)] = gd_all[k, cr * rings + d * per + s]

    def last_core(k):
        emb_core(18 + k, gd_all, k).wait_recv()
        put(k, 1)

    stages = [last_z, last_y, last_core]
    for step in range(chunks + len(stages) - 1):
        for late, stage in enumerate(stages):
            if 0 <= step - late < chunks:
                stage(step - late)

    for cp, when in unsent:
        if when is None:
            cp.wait_send()
        else:
            pl.when(when)(cp.wait_send)


def on_device(
    dims, inputs, positives, margins, neg_block, neg_row, block_home, bank, up_weight, up_bias,
    down_weight,
):
    nx, ny, nz, nc, cap = dims
    width = inputs.shape[1]
    half = width // 2
    units = up_weight.shape[1]
    queries = inputs.shape[0]
    per = min(4, nz)
    chunks = nz // per
    rings = ny * per
    block = nc * rings
    slots = cap * block
    gd_pieces = units // ny // 16
    V = pltpu.VMEM
    args = (
        inputs, positives, neg_block, neg_row, margins, block_home.reshape(1, -1), bank,
        up_weight, up_bias, down_weight,
    )
    scratch = [V(a.shape, a.dtype) for a in args] + [
        V((chunks, block, 1, 2 * PAIRS), F32),
        V((chunks, block, 16, half), BF16),
        V((chunks, block, 1, 128), F32),
        V((nc, queries, units), BF16),
        V((ny, units // ny, nc * queries), BF16),
        V((ny, units // ny, nc * queries), BF16),
        V((ny, nc, queries, half), BF16),
        V((chunks, block, 16, half), BF16),
        V((nx, 16, half), BF16),
        V((nx, 16, half), BF16),
        V((nx, 16, half), BF16),
        V((nx, 16, half), BF16),
        V((nc, nx, 16, half), BF16),
        V((nx, 16, half), F32),
        V((nx, 16, half), F32),
        V((queries, units), F32),
        V((chunks, block, PAIRS), F32),
        V((chunks, slots, width), BF16),
        V((chunks, slots, 1), F32),
        V((chunks, slots, 1), F32),
        V((chunks, rings, 16, half), F32),
        V((chunks, rings, 16, half), BF16),
        V((chunks, rings, 16, half), BF16),
        V((chunks, ny, per, 16, half), BF16),
        V((chunks, ny, per, 16, half), BF16),
        V((chunks, per, 16, half), BF16),
        V((nz, 16, half), BF16),
        V((chunks, rings, 1, 128), F32),
        V((chunks, rings, 1, 128), F32),
        V((chunks, rings, 1, 128), F32),
        V((chunks, ny, per, 1, 128), F32),
        V((chunks, ny, per, 1, 128), F32),
        V((chunks, per, 1, 128), F32),
        V((nz, 1, 128), F32),
        V((gd_pieces, 16, half), BF16),
        V((nz, 16, half), BF16),
        pltpu.SemaphoreType.DMA((len(args),)),
        pltpu.SemaphoreType.DMA((2, 4 * nx)),
        pltpu.SemaphoreType.DMA((2, 7 * nz)),
        pltpu.SemaphoreType.DMA((2, 23 * ny)),
        pltpu.SemaphoreType.DMA((2, 22)),
    ]
    vmem = pl.BlockSpec(memory_space=pltpu.VMEM)
    return pl.pallas_call(
        functools.partial(kernel, dims),
        out_shape=(
            pltpu.VMEM((QH, width), BF16),
            pltpu.VMEM((units, width), BF16),
        ),
        in_specs=[pl.BlockSpec(memory_space=pltpu.HBM)] * len(args),
        out_specs=(vmem, vmem),
        scratch_shapes=scratch,
        compiler_params=pltpu.CompilerParams(
            collective_id=0, has_side_effects=True, vmem_limit_bytes=60 * 1024 * 1024
        ),
        cost_estimate=pl.CostEstimate(
            flops=4_000_000_000, bytes_accessed=6_000_000, transcendentals=30_000
        ),
    )(*args)


def solution(mesh, ny=4, nc=2, cap=4):
    nx = mesh.shape["head"]
    nz = mesh.shape["bank"] // (ny * nc)
    return jax.shard_map(
        functools.partial(on_device, (nx, ny, nz, nc, cap)),
        mesh=mesh,
        in_specs=(
            P("bank", None),
            P("bank", None),
            P("bank", None),
            P("bank", None),
            P("bank", None),
            P(),
            P("bank", None),
            P(None, "head"),
            P("head"),
            P("head", None),
        ),
        out_specs=(P(("bank", "head"), None), P("head", None)),
        check_vma=False,
    )
```

```python
import functools
import math

import jax
import jax.numpy as jnp
from jax import lax
from jax.experimental import pallas as pl
from jax.experimental.pallas import tpu as pltpu
from jax.sharding import PartitionSpec as P

MESH = pl.DeviceIdType.MESH
F32 = jnp.float32
BF16 = jnp.bfloat16
I32 = jnp.int32
NEG = 32
BLOCK_ROWS = 128
QH = 8
PAIRS = QH * NEG
K0 = math.sqrt(2.0 / math.pi)
K1 = 0.044715


def iota(shape, axis):
    return lax.broadcasted_iota(I32, shape, axis)


def dot(a, b, ca=1, cb=0):
    return lax.dot_general(a, b, (((ca,), (cb,)), ((), ())), preferred_element_type=F32)


def fold(rows):
    w = rows.shape[1] // 2
    return jnp.concatenate([rows[:, :w], rows[:, w:]], axis=0)


def unfold(rows):
    return jnp.concatenate([rows[:QH], rows[QH:]], axis=1)


def kernel(
    dims,
    in_hbm, pos_hbm, nb_hbm, nr_hbm, mg_hbm, home_hbm, bank_hbm, up_hbm, bias_hbm, down_hbm,
    gi_ref, gd_ref,
    in_ref, pos_ref, nb_ref, nr_ref, mg_ref, home_ref, bank_ref, up_ref, bias_ref, down_ref,
    meta_all, e_all, ps_all, h_two, ht_send, ht_all, f_all, gd_all,
    xs, xr, xs2, xr2, xg, in_l, pos_l, dgelu,
    pm_sc, near_sc, q_sc, m_sc,
    g_own, g_send, gc_recv, gy_send, gy_recv, gz_send, gz_recv,
    r_own, r_send, rc_recv, ry_send, ry_recv, rz_send, rz_recv,
    p_sc, pz_recv,
    lsem, xsem, zsem, ysem, csem,
):
    nx, ny, nz, nc, cap = dims
    per = min(4, nz)
    chunks = nz // per
    rings = ny * per
    block = nc * rings
    slots = cap * block
    b = lax.axis_index("bank")
    x = lax.axis_index("head")
    c = lax.rem(b, nc)
    z = lax.rem(b // nc, nz)
    y = b // (nc * nz)
    oc = 1 - c
    width = in_ref.shape[1]
    half = width // 2
    units = up_ref.shape[1]
    rows_own = bank_ref.shape[0]
    homes = home_ref.shape[1]
    gd_pieces = units // ny // 16
    offs = [(s + 1) // 2 if s % 2 else -(s // 2) for s in range(nz)]

    def bid(yy, zz, cc):
        return (yy * nz + zz) * nc + cc

    def zat(off):
        return lax.rem(z + (off + nz), nz)

    def xdev(d):
        return (b, lax.rem(x + d, nx))

    def xcdev(d):
        return (bid(y, z, oc), lax.rem(x + d, nx))

    def zdev(off):
        return (bid(y, zat(off), c), x)

    def ydev(d):
        return (bid(lax.rem(y + d, ny), z, c), x)

    def piece_of(zz):
        return zz * gd_pieces // nz

    def owns(zz):
        return piece_of(zz + 1) > piece_of(zz)

    ys = sorted(range(1, ny), key=lambda d: -min(d, ny - d))
    xsd = sorted(range(1, nx), key=lambda d: -min(d, nx - d))
    cdev = xcdev(0)
    unsent = []

    def copy(src, dst, sems, i, dev):
        return pltpu.make_async_remote_copy(
            src_ref=src, dst_ref=dst, send_sem=sems.at[0, i], recv_sem=sems.at[1, i],
            device_id=dev, device_id_type=MESH,
        )

    def start(cp, when=None):
        if when is None:
            cp.start()
        else:
            pl.when(when)(cp.start)
        unsent.append((cp, when))

    def zcopy(k, s, off, src, dst):
        return copy(src, dst, zsem, k * nz + s, zdev(off))

    def ycopy(k, d, src, dst):
        return copy(src, dst, ysem, k * ny + d, ydev(d))

    def ccopy(k, src, dst):
        return copy(src, dst, csem, k, cdev)

    def xcopy(k, d, src, dst):
        return copy(src, dst, xsem, k * nx + d, xdev(d))

    pairs = [
        (in_hbm, in_ref), (up_hbm, up_ref), (bias_hbm, bias_ref), (down_hbm, down_ref),
        (nb_hbm, nb_ref), (nr_hbm, nr_ref), (mg_hbm, mg_ref), (home_hbm, home_ref),
        (pos_hbm, pos_ref), (bank_hbm, bank_ref),
    ]
    loads = [pltpu.make_async_copy(src, dst, lsem.at[i]) for i, (src, dst) in enumerate(pairs)]
    for cp in loads:
        cp.start()

    barrier = pltpu.get_barrier_semaphore()
    greet = [xcdev(d) for d in range(nx)] + [xdev(d) for d in range(1, nx)]
    greet += [ydev(d) for d in range(1, ny)] + []
    greet = [zdev(o) for o in offs[:0:-1]] + greet
    for dev in greet:
        pl.semaphore_signal(barrier, inc=1, device_id=dev, device_id_type=MESH)

    for cp in loads[:4]:
        cp.wait()
    queries = in_ref[...]
    pre = dot(queries, up_ref[...]) + bias_ref[...].reshape(1, units)
    t = jnp.tanh(K0 * (pre + K1 * (pre * pre * pre)))
    hid = (0.5 * pre * (1.0 + t)).astype(BF16)
    h_two[0] = hid
    partial = dot(hid, down_ref[...])
    for i in range(nx):
        xs[i] = fold(partial[QH * i:QH * (i + 1)]).astype(BF16)

    for cp in loads[4:8]:
        cp.wait()
    mine8 = pl.ds(pl.multiple_of(x * QH, QH), QH)
    lanes = 128 // NEG

    def row_of(rows, i):
        return jnp.concatenate([rows[lanes * i + k:lanes * i + k + 1] for k in range(lanes)], axis=1)

    home = home_ref[...]
    part = iota((8, homes), 0)
    home8 = jnp.broadcast_to(home, (8, homes))
    table = jnp.where(part == 0, home8 >> 1, jnp.where(part == 1, home8 & 1, 0))
    table = table.astype(F32).astype(BF16)
    nb8, nr8, mg8 = nb_ref[mine8, :], nr_ref[mine8, :], mg_ref[mine8, :]
    for i in range(PAIRS // 128):
        hot = jnp.where(iota((homes, 128), 0) == row_of(nb8, i), 1.0, 0.0).astype(BF16)
        found = dot(table, hot)
        place = 2.0 * found[0:1] + found[1:2]
        ids = place * float(BLOCK_ROWS) + row_of(nr8, i).astype(F32)
        meta_all[0, 0, :, pl.ds(128 * i, 128)] = ids
        meta_all[0, 0, :, pl.ds(PAIRS + 128 * i, 128)] = row_of(mg8, i)

    pl.semaphore_wait(barrier, len(greet))

    far_first = list(range(nz - 1, 0, -1))

    def zgather(k, s, ref):
        return zcopy(k, s, -offs[s], ref.at[0, pl.ds(0, 1)], ref.at[s // per, pl.ds(s % per, 1)])

    for d in xsd:
        start(xcopy(0, d, xs.at[lax.rem(x + d, nx)], xr.at[d]))
    for s in far_first:
        start(zgather(0, s, meta_all))
    start(ccopy(0, h_two.at[0], h_two.at[1]))
    dgelu[...] = 0.5 * (1.0 + t) + 0.5 * pre * (1.0 - t * t) * (K0 * (1.0 + 3.0 * K1 * (pre * pre)))
    inf = queries.astype(F32)
    loads[8].wait()
    posf = pos_ref[...].astype(F32)
    for i in range(nx):
        in_l[i] = fold(inf[QH * i:QH * (i + 1)])
        pos_l[i] = fold(posf[QH * i:QH * (i + 1)])

    total = xs[x].astype(F32)
    for d in range(1, nx):
        xcopy(0, d, xs.at[0], xr.at[d]).wait_recv()
        total = total + xr[d].astype(F32)
    emb = (in_l[x] + total).astype(BF16)
    e_all[0, 0] = emb
    s16 = jnp.sum(emb.astype(F32) * pos_l[x], axis=1, keepdims=True)
    s8 = s16[:QH] + s16[QH:]
    diag = iota((QH, 128), 0) == iota((QH, 128), 1)
    ps_all[0, 0] = jnp.sum(jnp.where(diag, s8, 0.0), axis=0, keepdims=True)
    for s in range(1, nz):
        start(zgather(1, s, e_all))
        start(zgather(2, s, ps_all))

    def near_ring(ref, k, d=0):
        return ref.at[k, pl.ds(d * per, per)]

    def emb_z(k):
        for s in range(max(1, k * per), (k + 1) * per):
            zgather(1, s, e_all).wait_recv()
            zgather(2, s, ps_all).wait_recv()
        for d in ys:
            start(ycopy(2 + k, d, near_ring(e_all, k), near_ring(e_all, k, ny - d)))
            start(ycopy(6 + k, d, near_ring(ps_all, k), near_ring(ps_all, k, ny - d)))

    def emb_y(k):
        for d in range(1, ny):
            ycopy(2 + k, d, near_ring(e_all, k), near_ring(e_all, k, ny - d)).wait_recv()
            ycopy(6 + k, d, near_ring(ps_all, k), near_ring(ps_all, k, ny - d)).wait_recv()
        start(emb_core(2 + k, e_all, k))
        start(emb_core(6 + k, ps_all, k))

    def emb_core(i, ref, k):
        return ccopy(i, ref.at[k, pl.ds(0, rings)], ref.at[k, pl.ds(rings, rings)])

    ccopy(0, h_two.at[0], h_two.at[1]).wait_recv()
    turned = jnp.concatenate([h_two[0].astype(F32), h_two[1].astype(F32)], axis=0).T
    ht_send[...] = turned.astype(BF16).reshape(ht_send.shape)
    for d in ys:
        start(ycopy(0, d, ht_send.at[lax.rem(y + d, ny)], ht_all.at[ny - d]))
    ht_all[0] = ht_send[y]

    for s in range(1, nz):
        zgather(0, s, meta_all).wait_recv()

    def meta_y(d):
        return ycopy(
            1, d, meta_all.at[:, pl.ds(0, per)], meta_all.at[:, pl.ds((ny - d) * per, per)]
        )

    for d in ys:
        start(meta_y(d))
    for d in range(1, ny):
        meta_y(d).wait_recv()
    meta_c = ccopy(1, meta_all.at[:, pl.ds(0, rings)], meta_all.at[:, pl.ds(rings, rings)])
    start(meta_c)
    emb_z(0)
    meta_c.wait_recv()
    loads[9].wait()

    tri = jnp.where(iota((PAIRS, PAIRS), 0) <= iota((PAIRS, PAIRS), 1), 1.0, 0.0).astype(BF16)
    q_lane = (iota((block, PAIRS), 1) // NEG + 1).astype(F32)
    def find(k):
        ids = meta_all[k, :, 0, pl.ds(0, PAIRS)].astype(I32)
        margins = meta_all[k, :, 0, pl.ds(PAIRS, PAIRS)]
        owner = ids // rows_own
        local = (ids - owner * rows_own).astype(F32)
        mine = owner == b
        prefix = dot(jnp.where(mine, 1.0, 0.0).astype(BF16), tri)
        pm = jnp.where(mine, prefix, 0.0)
        pm_sc[k] = pm
        rows, qs, ms = [], [], []
        for r in range(cap):
            sel = pm == float(r + 1)
            rows.append(jnp.sum(jnp.where(sel, local, 0.0), axis=1, keepdims=True))
            qs.append(jnp.sum(jnp.where(sel, q_lane, 0.0), axis=1, keepdims=True))
            ms.append(jnp.sum(jnp.where(sel, margins, 0.0), axis=1, keepdims=True))
        rows, qs = jnp.concatenate(rows, axis=0), jnp.concatenate(qs, axis=0)
        q_sc[k] = qs
        m_sc[k] = jnp.concatenate(ms, axis=0)
        row_i = jnp.where(qs > 0.5, rows, -1.0).astype(I32)
        hot_row = jnp.where(iota((slots, rows_own), 1) == row_i, 1.0, 0.0).astype(BF16)
        near_sc[k] = dot(hot_row, bank_ref[...]).astype(BF16)

    ind = jnp.where(iota((PAIRS, 128), 0) // NEG == iota((PAIRS, 128), 1), 1.0, 0.0).astype(BF16)

    def score(k):
        emb_core(2 + k, e_all, k).wait_recv()
        emb_core(6 + k, ps_all, k).wait_recv()
        qs = q_sc[k]
        q_i = qs.astype(I32) - 1
        ps_rep = jnp.concatenate([ps_all[k, :, 0, :]] * cap, axis=0)
        ps = jnp.sum(jnp.where(iota((slots, 128), 1) == q_i, ps_rep, 0.0), axis=1, keepdims=True)
        offsets = (ps - m_sc[k]).astype(BF16).astype(F32)
        group_i = lax.rem(iota((slots, 1), 0), block)
        target = jnp.where(qs > 0.5, group_i * 16 + q_i, -100)
        target = jnp.concatenate([target, target + QH], axis=0)
        hot_q = jnp.where(iota((2 * slots, block * 16), 1) == target, 1.0, 0.0).astype(BF16)
        embs = dot(hot_q, e_all[k].reshape(block * 16, half))
        near = near_sc[k].astype(F32)
        found = jnp.sum(
            embs[:slots] * near[:, :half] + embs[slots:] * near[:, half:], axis=1, keepdims=True
        )
        residual = offsets - found
        weighted = (residual * near).astype(BF16)
        weighted = jnp.concatenate([weighted[:, :half], weighted[:, half:]], axis=0)
        summed = dot(hot_q, weighted, 0, 0).reshape(block, 16, half)
        rounded = residual.astype(BF16).astype(F32)
        pm = pm_sc[k]
        per_pair = jnp.zeros((block, PAIRS), F32)
        for r in range(cap):
            per_pair = per_pair + jnp.where(
                pm == float(r + 1), rounded[r * block:(r + 1) * block], 0.0
            )
        rsum = dot(per_pair.astype(BF16), ind)
        g_send[k] = summed[rings:].astype(BF16)
        r_send[k, :, 0, :] = rsum[rings:]
        start(ccopy(10 + k, g_send.at[k], gc_recv.at[k]))
        start(ccopy(14 + k, r_send.at[k], rc_recv.at[k]))
        g_own[k] = summed[:rings]
        r_own[k, :, 0, :] = rsum[:rings]

    def sum_core(k):
        ccopy(10 + k, g_send.at[k], gc_recv.at[k]).wait_recv()
        ccopy(14 + k, r_send.at[k], rc_recv.at[k]).wait_recv()
        for d in ys + [0]:
            at = pl.ds(d * per, per)
            g_sum = g_own[k, at] + gc_recv[k, at].astype(F32)
            r_sum = r_own[k, at] + rc_recv[k, at]
            if d:
                gy_send[k, d] = g_sum.astype(BF16)
                ry_send[k, d] = r_sum
                start(ycopy(10 + k, d, gy_send.at[k, d], gy_recv.at[k, d]))
                start(ycopy(14 + k, d, ry_send.at[k, d], ry_recv.at[k, d]))
            else:
                g_own[k, at] = g_sum
                r_own[k, at] = r_sum

    def sum_y(k):
        g_sum = g_own[k, pl.ds(0, per)]
        r_sum = r_own[k, pl.ds(0, per)]
        for d in range(1, ny):
            ycopy(10 + k, d, gy_send.at[k, d], gy_recv.at[k, d]).wait_recv()
            ycopy(14 + k, d, ry_send.at[k, d], ry_recv.at[k, d]).wait_recv()
            g_sum = g_sum + gy_recv[k, d].astype(F32)
            r_sum = r_sum + ry_recv[k, d]
        gz_send[k] = g_sum.astype(BF16)
        rz_send[k] = r_sum
        if k == 0:
            g_own[0, 0] = g_sum[0]
        for s in range((k + 1) * per - 1, max(1, k * per) - 1, -1):
            start(zcopy(3, s, offs[s], gz_send.at[k, s % per], gz_recv.at[s]))
            start(zcopy(4, s, offs[s], rz_send.at[k, s % per], rz_recv.at[s]))

    if chunks == 4:
        order = [
            ("f", 0), ("f", 1), ("z", 1), ("y", 0), ("f", 2), ("z", 2), ("y", 1), ("s", 0),
            ("f", 3), ("s", 1), ("c", 0), ("z", 3), ("y", 2), ("c", 1), ("s", 2), ("a", 0),
            ("y", 3), ("c", 2), ("a", 1), ("s", 3), ("a", 2), ("c", 3), ("a", 3),
        ]
    else:
        order = [(name, k) for name in "fzysca" for k in range(chunks) if name + str(k) != "z0"]
    does = {"f": find, "z": emb_z, "y": emb_y, "s": score, "c": sum_core, "a": sum_y}
    for name, k in order:
        does[name](k)

    wsum = g_own[0, 0]
    rsum = rz_send[0, 0]
    for s in range(1, nz):
        zcopy(3, s, offs[s], gz_send.at[0, 0], gz_recv.at[s]).wait_recv()
        zcopy(4, s, offs[s], rz_send.at[0, 0], rz_recv.at[s]).wait_recv()
        wsum = wsum + gz_recv[s].astype(F32)
        rsum = rsum + rz_recv[s]
    lane_q = iota((16, 128), 1) == lax.rem(iota((16, 128), 0), QH)
    rcol = jnp.sum(jnp.where(lane_q, rsum, 0.0), axis=1, keepdims=True)
    gradient = 2.0 * pos_l[x] * rcol - 2.0 * wsum
    xg[0, x] = gradient.astype(BF16)
    for d in xsd:
        start(xcopy(1, d, xg.at[0, x], xg.at[0, x]))
    for d in range(nx):
        start(copy(xg.at[0, x], xg.at[1, x], xsem, 3 * nx + d, xcdev(d)))
    for d in range(nx):
        src = lax.rem(x + nx - d, nx)
        if d:
            xcopy(1, d, xg.at[0, x], xg.at[0, src]).wait_recv()
        copy(xg.at[0, x], xg.at[1, src], xsem, 3 * nx + d, xcdev(d)).wait_recv()

    def halves(cr):
        pieces = [xg[cr, i].astype(F32) for i in range(nx)]
        top = jnp.concatenate([p[:QH] for p in pieces], axis=0)
        low = jnp.concatenate([p[QH:] for p in pieces], axis=0)
        f_all[0, cr] = jnp.where(c == 0, top, low).astype(BF16)
        return top, low

    top, low = halves(0)
    halves(1)
    for d in ys:
        start(ycopy(18, d, f_all.at[0], f_all.at[ny - d]))

    down_sum = dot(ht_all[0], f_all[0].reshape(nc * nx * QH, half))
    for d in range(1, ny):
        ycopy(0, d, ht_send.at[0], ht_all.at[ny - d]).wait_recv()
        ycopy(18, d, f_all.at[0], f_all.at[ny - d]).wait_recv()
        down_sum = down_sum + dot(ht_all[ny - d], f_all[ny - d].reshape(nc * nx * QH, half))
    p_sc[...] = down_sum.astype(BF16).reshape(gd_pieces, 16, half)
    for s in far_first:
        zz = zat(offs[s])
        start(zcopy(5, s, offs[s], p_sc.at[piece_of(zz)], pz_recv.at[s]), owns(zz))

    grad_all = jnp.concatenate([top, low], axis=1).astype(BF16)
    hidden_grad = dot(grad_all, down_ref[...], 1, 1)
    pre_grad = (hidden_grad * dgelu[...]).astype(BF16)
    carried = dot(pre_grad, up_ref[...], 1, 1)
    for i in range(nx):
        xs2[i] = fold(carried[QH * i:QH * (i + 1)]).astype(BF16)
    for d in xsd:
        start(xcopy(2, d, xs2.at[lax.rem(x + d, nx)], xr2.at[d]))

    busy = owns(z)
    scale = 1.0 / math.sqrt(nx * QH * ny * nz * nc)

    @pl.when(busy)
    def _():
        acc = p_sc[piece_of(z)].astype(F32)
        for s in range(1, nz):
            zcopy(5, s, offs[s], p_sc.at[0], pz_recv.at[s]).wait_recv()
            acc = acc + pz_recv[s].astype(F32)
        gd_all[0, 0] = (acc * scale).astype(BF16)

    def zlast(s):
        return zgather(6, s, gd_all)

    for s in range(1, nz):
        start(zlast(s), busy)

    carry = xs2[x].astype(F32) + gradient
    for d in range(1, nx):
        xcopy(2, d, xs2.at[0], xr2.at[d]).wait_recv()
        carry = carry + xr2[d].astype(F32)
    gi_ref[...] = unfold(carry).astype(BF16)

    def last_z(k):
        for s in range(max(1, k * per), (k + 1) * per):
            pl.when(owns(zat(offs[s])))(zlast(s).wait_recv)
        for d in ys:
            start(ycopy(19 + k, d, near_ring(gd_all, k), near_ring(gd_all, k, ny - d)))

    def last_y(k):
        for d in range(1, ny):
            ycopy(19 + k, d, near_ring(gd_all, k), near_ring(gd_all, k, ny - d)).wait_recv()
        start(emb_core(18 + k, gd_all, k))
        put(k, 0)

    def put(k, cr):
        at = c if cr == 0 else oc
        for s in range(per):
            zz = zat(offs[k * per + s])

            @pl.when(owns(zz))
            def _():
                for d in range(ny):
                    yy = lax.rem(y + d, ny)
                    row = pl.multiple_of((yy * gd_pieces + piece_of(zz)) * 16, 16)
                    col = pl.multiple_of(at * half, 128)
                    gd_ref[pl.ds(row, 16), pl.ds(col, half)] = gd_all[k, cr * rings + d * per + s]

    def last_core(k):
        emb_core(18 + k, gd_all, k).wait_recv()
        put(k, 1)

    stages = [last_z, last_y, last_core]
    for step in range(chunks + len(stages) - 1):
        for late, stage in enumerate(stages):
            if 0 <= step - late < chunks:
                stage(step - late)

    for cp, when in unsent:
        if when is None:
            cp.wait_send()
        else:
            pl.when(when)(cp.wait_send)


def on_device(
    dims, inputs, positives, margins, neg_block, neg_row, block_home, bank, up_weight, up_bias,
    down_weight,
):
    nx, ny, nz, nc, cap = dims
    width = inputs.shape[1]
    half = width // 2
    units = up_weight.shape[1]
    queries = inputs.shape[0]
    per = min(4, nz)
    chunks = nz // per
    rings = ny * per
    block = nc * rings
    slots = cap * block
    gd_pieces = units // ny // 16
    V = pltpu.VMEM
    args = (
        inputs, positives, neg_block, neg_row, margins, block_home.reshape(1, -1), bank,
        up_weight, up_bias, down_weight,
    )
    scratch = [V(a.shape, a.dtype) for a in args] + [
        V((chunks, block, 1, 2 * PAIRS), F32),
        V((chunks, block, 16, half), BF16),
        V((chunks, block, 1, 128), F32),
        V((nc, queries, units), BF16),
        V((ny, units // ny, nc * queries), BF16),
        V((ny, units // ny, nc * queries), BF16),
        V((ny, nc, queries, half), BF16),
        V((chunks, block, 16, half), BF16),
        V((nx, 16, half), BF16),
        V((nx, 16, half), BF16),
        V((nx, 16, half), BF16),
        V((nx, 16, half), BF16),
        V((nc, nx, 16, half), BF16),
        V((nx, 16, half), F32),
        V((nx, 16, half), F32),
        V((queries, units), F32),
        V((chunks, block, PAIRS), F32),
        V((chunks, slots, width), BF16),
        V((chunks, slots, 1), F32),
        V((chunks, slots, 1), F32),
        V((chunks, rings, 16, half), F32),
        V((chunks, rings, 16, half), BF16),
        V((chunks, rings, 16, half), BF16),
        V((chunks, ny, per, 16, half), BF16),
        V((chunks, ny, per, 16, half), BF16),
        V((chunks, per, 16, half), BF16),
        V((nz, 16, half), BF16),
        V((chunks, rings, 1, 128), F32),
        V((chunks, rings, 1, 128), F32),
        V((chunks, rings, 1, 128), F32),
        V((chunks, ny, per, 1, 128), F32),
        V((chunks, ny, per, 1, 128), F32),
        V((chunks, per, 1, 128), F32),
        V((nz, 1, 128), F32),
        V((gd_pieces, 16, half), BF16),
        V((nz, 16, half), BF16),
        pltpu.SemaphoreType.DMA((len(args),)),
        pltpu.SemaphoreType.DMA((2, 4 * nx)),
        pltpu.SemaphoreType.DMA((2, 7 * nz)),
        pltpu.SemaphoreType.DMA((2, 23 * ny)),
        pltpu.SemaphoreType.DMA((2, 22)),
    ]
    vmem = pl.BlockSpec(memory_space=pltpu.VMEM)
    return pl.pallas_call(
        functools.partial(kernel, dims),
        out_shape=(
            pltpu.VMEM((QH, width), BF16),
            pltpu.VMEM((units, width), BF16),
        ),
        in_specs=[pl.BlockSpec(memory_space=pltpu.HBM)] * len(args),
        out_specs=(vmem, vmem),
        scratch_shapes=scratch,
        compiler_params=pltpu.CompilerParams(
            collective_id=0, has_side_effects=True, vmem_limit_bytes=60 * 1024 * 1024
        ),
        cost_estimate=pl.CostEstimate(
            flops=4_000_000_000, bytes_accessed=6_000_000, transcendentals=30_000
        ),
    )(*args)


def solution(mesh, ny=4, nc=2, cap=4):
    nx = mesh.shape["head"]
    nz = mesh.shape["bank"] // (ny * nc)
    return jax.shard_map(
        functools.partial(on_device, (nx, ny, nz, nc, cap)),
        mesh=mesh,
        in_specs=(
            P("bank", None),
            P("bank", None),
            P("bank", None),
            P("bank", None),
            P("bank", None),
            P(),
            P("bank", None),
            P(None, "head"),
            P("head"),
            P("head", None),
        ),
        out_specs=(P(("bank", "head"), None), P("head", None)),
        check_vma=False,
    )
```

```python
import functools
import math

import jax
import jax.numpy as jnp
from jax import lax
from jax.experimental import pallas as pl
from jax.experimental.pallas import tpu as pltpu
from jax.sharding import PartitionSpec as P

MESH = pl.DeviceIdType.MESH
F32 = jnp.float32
BF16 = jnp.bfloat16
I32 = jnp.int32
NEG = 32
BLOCK_ROWS = 128
QH = 8
PAIRS = QH * NEG
K0 = math.sqrt(2.0 / math.pi)
K1 = 0.044715


def iota(shape, axis):
    return lax.broadcasted_iota(I32, shape, axis)


def dot(a, b, ca=1, cb=0):
    return lax.dot_general(a, b, (((ca,), (cb,)), ((), ())), preferred_element_type=F32)


def fold(rows):
    w = rows.shape[1] // 2
    return jnp.concatenate([rows[:, :w], rows[:, w:]], axis=0)


def unfold(rows):
    return jnp.concatenate([rows[:QH], rows[QH:]], axis=1)


def kernel(
    dims,
    in_hbm, pos_hbm, nb_hbm, nr_hbm, mg_hbm, home_hbm, bank_hbm, up_hbm, bias_hbm, down_hbm,
    gi_ref, gd_ref,
    in_ref, pos_ref, nb_ref, nr_ref, mg_ref, home_ref, bank_ref, up_ref, bias_ref, down_ref,
    meta_all, e_all, ps_all, h_two, ht_send, ht_all, f_all, gd_all,
    xs, xr, xs2, xr2, xg, in_l, pos_l, dgelu,
    pm_sc, near_sc, q_sc, m_sc,
    g_own, g_send, gc_recv, gy_send, gy_recv, gz_send, gz_recv,
    r_own, r_send, rc_recv, ry_send, ry_recv, rz_send, rz_recv,
    p_sc, pz_recv,
    lsem, xsem, zsem, ysem, csem,
):
    nx, ny, nz, nc, cap = dims
    per = min(4, nz)
    chunks = nz // per
    rings = ny * per
    block = nc * rings
    slots = cap * block
    b = lax.axis_index("bank")
    x = lax.axis_index("head")
    c = lax.rem(b, nc)
    z = lax.rem(b // nc, nz)
    y = b // (nc * nz)
    oc = 1 - c
    width = in_ref.shape[1]
    half = width // 2
    units = up_ref.shape[1]
    rows_own = bank_ref.shape[0]
    homes = home_ref.shape[1]
    gd_pieces = units // ny // 16
    offs = [(s + 1) // 2 if s % 2 else -(s // 2) for s in range(nz)]

    def bid(yy, zz, cc):
        return (yy * nz + zz) * nc + cc

    def zat(off):
        return lax.rem(z + (off + nz), nz)

    def xdev(d):
        return (b, lax.rem(x + d, nx))

    def xcdev(d):
        return (bid(y, z, oc), lax.rem(x + d, nx))

    def zdev(off):
        return (bid(y, zat(off), c), x)

    def ydev(d):
        return (bid(lax.rem(y + d, ny), z, c), x)

    def piece_of(zz):
        return zz * gd_pieces // nz

    def owns(zz):
        return piece_of(zz + 1) > piece_of(zz)

    ys = sorted(range(1, ny), key=lambda d: -min(d, ny - d))
    xsd = sorted(range(1, nx), key=lambda d: -min(d, nx - d))
    cdev = xcdev(0)
    unsent = []

    def copy(src, dst, sems, i, dev):
        return pltpu.make_async_remote_copy(
            src_ref=src, dst_ref=dst, send_sem=sems.at[0, i], recv_sem=sems.at[1, i],
            device_id=dev, device_id_type=MESH,
        )

    def start(cp, when=None):
        if when is None:
            cp.start()
        else:
            pl.when(when)(cp.start)
        unsent.append((cp, when))

    def drain(count):
        for cp, when in unsent[:count]:
            if when is None:
                cp.wait_send()
            else:
                pl.when(when)(cp.wait_send)
        del unsent[:count]

    def zcopy(k, s, off, src, dst):
        return copy(src, dst, zsem, k * nz + s, zdev(off))

    def ycopy(k, d, src, dst):
        return copy(src, dst, ysem, k * ny + d, ydev(d))

    def ccopy(k, src, dst):
        return copy(src, dst, csem, k, cdev)

    def xcopy(k, d, src, dst):
        return copy(src, dst, xsem, k * nx + d, xdev(d))

    pairs = [
        (in_hbm, in_ref), (up_hbm, up_ref), (bias_hbm, bias_ref), (down_hbm, down_ref),
        (nb_hbm, nb_ref), (nr_hbm, nr_ref), (mg_hbm, mg_ref), (home_hbm, home_ref),
        (pos_hbm, pos_ref), (bank_hbm, bank_ref),
    ]
    loads = [pltpu.make_async_copy(src, dst, lsem.at[i]) for i, (src, dst) in enumerate(pairs)]
    for cp in loads:
        cp.start()

    barrier = pltpu.get_barrier_semaphore()
    greet = [xcdev(d) for d in range(nx)] + [xdev(d) for d in range(1, nx)]
    greet += [ydev(d) for d in range(1, ny)] + []
    greet = [zdev(o) for o in offs[:0:-1]] + greet
    for dev in greet:
        pl.semaphore_signal(barrier, inc=1, device_id=dev, device_id_type=MESH)

    for cp in loads[:4]:
        cp.wait()
    queries = in_ref[...]
    pre = dot(queries, up_ref[...]) + bias_ref[...].reshape(1, units)
    t = jnp.tanh(K0 * (pre + K1 * (pre * pre * pre)))
    hid = (0.5 * pre * (1.0 + t)).astype(BF16)
    h_two[0] = hid
    partial = dot(hid, down_ref[...])
    for i in range(nx):
        xs[i] = fold(partial[QH * i:QH * (i + 1)]).astype(BF16)

    for cp in loads[4:8]:
        cp.wait()
    mine8 = pl.ds(pl.multiple_of(x * QH, QH), QH)
    lanes = 128 // NEG

    def row_of(rows, i):
        return jnp.concatenate([rows[lanes * i + k:lanes * i + k + 1] for k in range(lanes)], axis=1)

    home = home_ref[...]
    part = iota((8, homes), 0)
    home8 = jnp.broadcast_to(home, (8, homes))
    table = jnp.where(part == 0, home8 >> 1, jnp.where(part == 1, home8 & 1, 0))
    table = table.astype(F32).astype(BF16)
    nb8, nr8, mg8 = nb_ref[mine8, :], nr_ref[mine8, :], mg_ref[mine8, :]
    for i in range(PAIRS // 128):
        hot = jnp.where(iota((homes, 128), 0) == row_of(nb8, i), 1.0, 0.0).astype(BF16)
        found = dot(table, hot)
        place = 2.0 * found[0:1] + found[1:2]
        ids = place * float(BLOCK_ROWS) + row_of(nr8, i).astype(F32)
        meta_all[0, 0, :, pl.ds(128 * i, 128)] = ids
        meta_all[0, 0, :, pl.ds(PAIRS + 128 * i, 128)] = row_of(mg8, i)

    pl.semaphore_wait(barrier, len(greet))

    far_first = list(range(nz - 1, 0, -1))

    def zgather(k, s, ref):
        return zcopy(k, s, -offs[s], ref.at[0, pl.ds(0, 1)], ref.at[s // per, pl.ds(s % per, 1)])

    for d in xsd:
        start(xcopy(0, d, xs.at[lax.rem(x + d, nx)], xr.at[d]))
    for s in far_first:
        start(zgather(0, s, meta_all))
    start(ccopy(0, h_two.at[0], h_two.at[1]))
    dgelu[...] = 0.5 * (1.0 + t) + 0.5 * pre * (1.0 - t * t) * (K0 * (1.0 + 3.0 * K1 * (pre * pre)))
    inf = queries.astype(F32)
    loads[8].wait()
    posf = pos_ref[...].astype(F32)
    for i in range(nx):
        in_l[i] = fold(inf[QH * i:QH * (i + 1)])
        pos_l[i] = fold(posf[QH * i:QH * (i + 1)])

    total = xs[x].astype(F32)
    for d in range(1, nx):
        xcopy(0, d, xs.at[0], xr.at[d]).wait_recv()
        total = total + xr[d].astype(F32)
    emb = (in_l[x] + total).astype(BF16)
    e_all[0, 0] = emb
    s16 = jnp.sum(emb.astype(F32) * pos_l[x], axis=1, keepdims=True)
    s8 = s16[:QH] + s16[QH:]
    diag = iota((QH, 128), 0) == iota((QH, 128), 1)
    ps_all[0, 0] = jnp.sum(jnp.where(diag, s8, 0.0), axis=0, keepdims=True)
    for s in range(1, nz):
        start(zgather(1, s, e_all))
        start(zgather(2, s, ps_all))

    def near_ring(ref, k, d=0):
        return ref.at[k, pl.ds(d * per, per)]

    def emb_z(k):
        for s in range(max(1, k * per), (k + 1) * per):
            zgather(1, s, e_all).wait_recv()
            zgather(2, s, ps_all).wait_recv()
        for d in ys:
            start(ycopy(2 + k, d, near_ring(e_all, k), near_ring(e_all, k, ny - d)))
            start(ycopy(6 + k, d, near_ring(ps_all, k), near_ring(ps_all, k, ny - d)))

    def emb_y(k):
        for d in range(1, ny):
            ycopy(2 + k, d, near_ring(e_all, k), near_ring(e_all, k, ny - d)).wait_recv()
            ycopy(6 + k, d, near_ring(ps_all, k), near_ring(ps_all, k, ny - d)).wait_recv()
        start(emb_core(2 + k, e_all, k))
        start(emb_core(6 + k, ps_all, k))

    def emb_core(i, ref, k):
        return ccopy(i, ref.at[k, pl.ds(0, rings)], ref.at[k, pl.ds(rings, rings)])

    for s in range(1, nz):
        zgather(0, s, meta_all).wait_recv()

    def meta_y(d):
        return ycopy(
            1, d, meta_all.at[:, pl.ds(0, per)], meta_all.at[:, pl.ds((ny - d) * per, per)]
        )

    for d in ys:
        start(meta_y(d))
    for d in range(1, ny):
        meta_y(d).wait_recv()
    meta_c = ccopy(1, meta_all.at[:, pl.ds(0, rings)], meta_all.at[:, pl.ds(rings, rings)])
    start(meta_c)
    emb_z(0)
    meta_c.wait_recv()
    loads[9].wait()

    tri = jnp.where(iota((PAIRS, PAIRS), 0) <= iota((PAIRS, PAIRS), 1), 1.0, 0.0).astype(BF16)
    q_lane = (iota((block, PAIRS), 1) // NEG + 1).astype(F32)
    def find(k):
        ids = meta_all[k, :, 0, pl.ds(0, PAIRS)].astype(I32)
        margins = meta_all[k, :, 0, pl.ds(PAIRS, PAIRS)]
        owner = ids // rows_own
        local = (ids - owner * rows_own).astype(F32)
        mine = owner == b
        prefix = dot(jnp.where(mine, 1.0, 0.0).astype(BF16), tri)
        pm = jnp.where(mine, prefix, 0.0)
        pm_sc[k] = pm
        rows, qs, ms = [], [], []
        for r in range(cap):
            sel = pm == float(r + 1)
            rows.append(jnp.sum(jnp.where(sel, local, 0.0), axis=1, keepdims=True))
            qs.append(jnp.sum(jnp.where(sel, q_lane, 0.0), axis=1, keepdims=True))
            ms.append(jnp.sum(jnp.where(sel, margins, 0.0), axis=1, keepdims=True))
        rows, qs = jnp.concatenate(rows, axis=0), jnp.concatenate(qs, axis=0)
        q_sc[k] = qs
        m_sc[k] = jnp.concatenate(ms, axis=0)
        row_i = jnp.where(qs > 0.5, rows, -1.0).astype(I32)
        hot_row = jnp.where(iota((slots, rows_own), 1) == row_i, 1.0, 0.0).astype(BF16)
        near_sc[k] = dot(hot_row, bank_ref[...]).astype(BF16)

    ind = jnp.where(iota((PAIRS, 128), 0) // NEG == iota((PAIRS, 128), 1), 1.0, 0.0).astype(BF16)

    def score(k):
        emb_core(2 + k, e_all, k).wait_recv()
        emb_core(6 + k, ps_all, k).wait_recv()
        qs = q_sc[k]
        q_i = qs.astype(I32) - 1
        ps_rep = jnp.concatenate([ps_all[k, :, 0, :]] * cap, axis=0)
        ps = jnp.sum(jnp.where(iota((slots, 128), 1) == q_i, ps_rep, 0.0), axis=1, keepdims=True)
        offsets = (ps - m_sc[k]).astype(BF16).astype(F32)
        group_i = lax.rem(iota((slots, 1), 0), block)
        target = jnp.where(qs > 0.5, group_i * 16 + q_i, -100)
        target = jnp.concatenate([target, target + QH], axis=0)
        hot_q = jnp.where(iota((2 * slots, block * 16), 1) == target, 1.0, 0.0).astype(BF16)
        embs = dot(hot_q, e_all[k].reshape(block * 16, half))
        near = near_sc[k].astype(F32)
        found = jnp.sum(
            embs[:slots] * near[:, :half] + embs[slots:] * near[:, half:], axis=1, keepdims=True
        )
        residual = offsets - found
        weighted = (residual * near).astype(BF16)
        weighted = jnp.concatenate([weighted[:, :half], weighted[:, half:]], axis=0)
        summed = dot(hot_q, weighted, 0, 0).reshape(block, 16, half)
        rounded = residual.astype(BF16).astype(F32)
        pm = pm_sc[k]
        per_pair = jnp.zeros((block, PAIRS), F32)
        for r in range(cap):
            per_pair = per_pair + jnp.where(
                pm == float(r + 1), rounded[r * block:(r + 1) * block], 0.0
            )
        rsum = dot(per_pair.astype(BF16), ind)
        g_send[k] = summed[rings:].astype(BF16)
        r_send[k, :, 0, :] = rsum[rings:]
        start(ccopy(10 + k, g_send.at[k], gc_recv.at[k]))
        start(ccopy(14 + k, r_send.at[k], rc_recv.at[k]))
        g_own[k] = summed[:rings]
        r_own[k, :, 0, :] = rsum[:rings]

    def sum_core(k):
        ccopy(10 + k, g_send.at[k], gc_recv.at[k]).wait_recv()
        ccopy(14 + k, r_send.at[k], rc_recv.at[k]).wait_recv()
        for d in ys + [0]:
            at = pl.ds(d * per, per)
            g_sum = g_own[k, at] + gc_recv[k, at].astype(F32)
            r_sum = r_own[k, at] + rc_recv[k, at]
            if d:
                gy_send[k, d] = g_sum.astype(BF16)
                ry_send[k, d] = r_sum
                start(ycopy(10 + k, d, gy_send.at[k, d], gy_recv.at[k, d]))
                start(ycopy(14 + k, d, ry_send.at[k, d], ry_recv.at[k, d]))
            else:
                g_own[k, at] = g_sum
                r_own[k, at] = r_sum

    def sum_y(k):
        g_sum = g_own[k, pl.ds(0, per)]
        r_sum = r_own[k, pl.ds(0, per)]
        for d in range(1, ny):
            ycopy(10 + k, d, gy_send.at[k, d], gy_recv.at[k, d]).wait_recv()
            ycopy(14 + k, d, ry_send.at[k, d], ry_recv.at[k, d]).wait_recv()
            g_sum = g_sum + gy_recv[k, d].astype(F32)
            r_sum = r_sum + ry_recv[k, d]
        gz_send[k] = g_sum.astype(BF16)
        rz_send[k] = r_sum
        if k == 0:
            g_own[0, 0] = g_sum[0]
        for s in range((k + 1) * per - 1, max(1, k * per) - 1, -1):
            start(zcopy(3, s, offs[s], gz_send.at[k, s % per], gz_recv.at[s]))
            start(zcopy(4, s, offs[s], rz_send.at[k, s % per], rz_recv.at[s]))

    if chunks == 4:
        order = [
            ("f", 0), ("f", 1), ("z", 1), ("y", 0), ("f", 2), ("z", 2), ("y", 1), ("s", 0),
            ("f", 3), ("s", 1), ("c", 0), ("z", 3), ("y", 2), ("c", 1), ("s", 2), ("a", 0),
            ("y", 3), ("c", 2), ("a", 1), ("s", 3), ("a", 2), ("c", 3), ("a", 3),
        ]
    else:
        order = [(name, k) for name in "fzysca" for k in range(chunks) if name + str(k) != "z0"]
    does = {"f": find, "z": emb_z, "y": emb_y, "s": score, "c": sum_core, "a": sum_y}
    for name, k in order:
        does[name](k)

    ccopy(0, h_two.at[0], h_two.at[1]).wait_recv()
    turned = jnp.concatenate([h_two[0].astype(F32), h_two[1].astype(F32)], axis=0).T
    ht_send[...] = turned.astype(BF16).reshape(ht_send.shape)
    for d in ys:
        start(ycopy(0, d, ht_send.at[lax.rem(y + d, ny)], ht_all.at[ny - d]))
    ht_all[0] = ht_send[y]

    wsum = g_own[0, 0]
    rsum = rz_send[0, 0]
    for s in range(1, nz):
        zcopy(3, s, offs[s], gz_send.at[0, 0], gz_recv.at[s]).wait_recv()
        zcopy(4, s, offs[s], rz_send.at[0, 0], rz_recv.at[s]).wait_recv()
        wsum = wsum + gz_recv[s].astype(F32)
        rsum = rsum + rz_recv[s]
    lane_q = iota((16, 128), 1) == lax.rem(iota((16, 128), 0), QH)
    rcol = jnp.sum(jnp.where(lane_q, rsum, 0.0), axis=1, keepdims=True)
    gradient = 2.0 * pos_l[x] * rcol - 2.0 * wsum
    xg[0, x] = gradient.astype(BF16)
    for d in xsd:
        start(xcopy(1, d, xg.at[0, x], xg.at[0, x]))
    for d in range(nx):
        start(copy(xg.at[0, x], xg.at[1, x], xsem, 3 * nx + d, xcdev(d)))
    for d in range(nx):
        src = lax.rem(x + nx - d, nx)
        if d:
            xcopy(1, d, xg.at[0, x], xg.at[0, src]).wait_recv()
        copy(xg.at[0, x], xg.at[1, src], xsem, 3 * nx + d, xcdev(d)).wait_recv()

    def halves(cr):
        pieces = [xg[cr, i].astype(F32) for i in range(nx)]
        top = jnp.concatenate([p[:QH] for p in pieces], axis=0)
        low = jnp.concatenate([p[QH:] for p in pieces], axis=0)
        f_all[0, cr] = jnp.where(c == 0, top, low).astype(BF16)
        return top, low

    top, low = halves(0)
    halves(1)
    for d in ys:
        start(ycopy(18, d, f_all.at[0], f_all.at[ny - d]))

    older = len(unsent)
    down_sum = dot(ht_all[0], f_all[0].reshape(nc * nx * QH, half))
    for d in range(1, ny):
        ycopy(0, d, ht_send.at[0], ht_all.at[ny - d]).wait_recv()
        ycopy(18, d, f_all.at[0], f_all.at[ny - d]).wait_recv()
        down_sum = down_sum + dot(ht_all[ny - d], f_all[ny - d].reshape(nc * nx * QH, half))
    p_sc[...] = down_sum.astype(BF16).reshape(gd_pieces, 16, half)
    for s in far_first:
        zz = zat(offs[s])
        start(zcopy(5, s, offs[s], p_sc.at[piece_of(zz)], pz_recv.at[s]), owns(zz))

    grad_all = jnp.concatenate([top, low], axis=1).astype(BF16)
    hidden_grad = dot(grad_all, down_ref[...], 1, 1)
    pre_grad = (hidden_grad * dgelu[...]).astype(BF16)
    carried = dot(pre_grad, up_ref[...], 1, 1)
    for i in range(nx):
        xs2[i] = fold(carried[QH * i:QH * (i + 1)]).astype(BF16)
    for d in xsd:
        start(xcopy(2, d, xs2.at[lax.rem(x + d, nx)], xr2.at[d]))

    drain(older)
    busy = owns(z)
    scale = 1.0 / math.sqrt(nx * QH * ny * nz * nc)

    @pl.when(busy)
    def _():
        acc = p_sc[piece_of(z)].astype(F32)
        for s in range(1, nz):
            zcopy(5, s, offs[s], p_sc.at[0], pz_recv.at[s]).wait_recv()
            acc = acc + pz_recv[s].astype(F32)
        gd_all[0, 0] = (acc * scale).astype(BF16)

    def zlast(s):
        return zgather(6, s, gd_all)

    for s in range(1, nz):
        start(zlast(s), busy)

    carry = xs2[x].astype(F32) + gradient
    for d in range(1, nx):
        xcopy(2, d, xs2.at[0], xr2.at[d]).wait_recv()
        carry = carry + xr2[d].astype(F32)
    gi_ref[...] = unfold(carry).astype(BF16)

    def last_z(k):
        for s in range(max(1, k * per), (k + 1) * per):
            pl.when(owns(zat(offs[s])))(zlast(s).wait_recv)
        for d in ys:
            start(ycopy(19 + k, d, near_ring(gd_all, k), near_ring(gd_all, k, ny - d)))

    def last_y(k):
        for d in range(1, ny):
            ycopy(19 + k, d, near_ring(gd_all, k), near_ring(gd_all, k, ny - d)).wait_recv()
        start(emb_core(18 + k, gd_all, k))
        put(k, 0)

    def put(k, cr):
        at = c if cr == 0 else oc
        for s in range(per):
            zz = zat(offs[k * per + s])

            @pl.when(owns(zz))
            def _():
                for d in range(ny):
                    yy = lax.rem(y + d, ny)
                    row = pl.multiple_of((yy * gd_pieces + piece_of(zz)) * 16, 16)
                    col = pl.multiple_of(at * half, 128)
                    gd_ref[pl.ds(row, 16), pl.ds(col, half)] = gd_all[k, cr * rings + d * per + s]

    def last_core(k):
        emb_core(18 + k, gd_all, k).wait_recv()
        put(k, 1)

    stages = [last_z, last_y, last_core]
    for step in range(chunks + len(stages) - 1):
        for late, stage in enumerate(stages):
            if 0 <= step - late < chunks:
                stage(step - late)

    drain(len(unsent))


def on_device(
    dims, inputs, positives, margins, neg_block, neg_row, block_home, bank, up_weight, up_bias,
    down_weight,
):
    nx, ny, nz, nc, cap = dims
    width = inputs.shape[1]
    half = width // 2
    units = up_weight.shape[1]
    queries = inputs.shape[0]
    per = min(4, nz)
    chunks = nz // per
    rings = ny * per
    block = nc * rings
    slots = cap * block
    gd_pieces = units // ny // 16
    V = pltpu.VMEM
    args = (
        inputs, positives, neg_block, neg_row, margins, block_home.reshape(1, -1), bank,
        up_weight, up_bias, down_weight,
    )
    scratch = [V(a.shape, a.dtype) for a in args] + [
        V((chunks, block, 1, 2 * PAIRS), F32),
        V((chunks, block, 16, half), BF16),
        V((chunks, block, 1, 128), F32),
        V((nc, queries, units), BF16),
        V((ny, units // ny, nc * queries), BF16),
        V((ny, units // ny, nc * queries), BF16),
        V((ny, nc, queries, half), BF16),
        V((chunks, block, 16, half), BF16),
        V((nx, 16, half), BF16),
        V((nx, 16, half), BF16),
        V((nx, 16, half), BF16),
        V((nx, 16, half), BF16),
        V((nc, nx, 16, half), BF16),
        V((nx, 16, half), F32),
        V((nx, 16, half), F32),
        V((queries, units), F32),
        V((chunks, block, PAIRS), F32),
        V((chunks, slots, width), BF16),
        V((chunks, slots, 1), F32),
        V((chunks, slots, 1), F32),
        V((chunks, rings, 16, half), F32),
        V((chunks, rings, 16, half), BF16),
        V((chunks, rings, 16, half), BF16),
        V((chunks, ny, per, 16, half), BF16),
        V((chunks, ny, per, 16, half), BF16),
        V((chunks, per, 16, half), BF16),
        V((nz, 16, half), BF16),
        V((chunks, rings, 1, 128), F32),
        V((chunks, rings, 1, 128), F32),
        V((chunks, rings, 1, 128), F32),
        V((chunks, ny, per, 1, 128), F32),
        V((chunks, ny, per, 1, 128), F32),
        V((chunks, per, 1, 128), F32),
        V((nz, 1, 128), F32),
        V((gd_pieces, 16, half), BF16),
        V((nz, 16, half), BF16),
        pltpu.SemaphoreType.DMA((len(args),)),
        pltpu.SemaphoreType.DMA((2, 4 * nx)),
        pltpu.SemaphoreType.DMA((2, 7 * nz)),
        pltpu.SemaphoreType.DMA((2, 23 * ny)),
        pltpu.SemaphoreType.DMA((2, 22)),
    ]
    vmem = pl.BlockSpec(memory_space=pltpu.VMEM)
    return pl.pallas_call(
        functools.partial(kernel, dims),
        out_shape=(
            pltpu.VMEM((QH, width), BF16),
            pltpu.VMEM((units, width), BF16),
        ),
        in_specs=[pl.BlockSpec(memory_space=pltpu.HBM)] * len(args),
        out_specs=(vmem, vmem),
        scratch_shapes=scratch,
        compiler_params=pltpu.CompilerParams(
            collective_id=0, has_side_effects=True, vmem_limit_bytes=60 * 1024 * 1024
        ),
        cost_estimate=pl.CostEstimate(
            flops=4_000_000_000, bytes_accessed=6_000_000, transcendentals=30_000
        ),
    )(*args)


def solution(mesh, ny=4, nc=2, cap=4):
    nx = mesh.shape["head"]
    nz = mesh.shape["bank"] // (ny * nc)
    return jax.shard_map(
        functools.partial(on_device, (nx, ny, nz, nc, cap)),
        mesh=mesh,
        in_specs=(
            P("bank", None),
            P("bank", None),
            P("bank", None),
            P("bank", None),
            P("bank", None),
            P(),
            P("bank", None),
            P(None, "head"),
            P("head"),
            P("head", None),
        ),
        out_specs=(P(("bank", "head"), None), P("head", None)),
        check_vma=False,
    )
```

```python
import functools
import math

import jax
import jax.numpy as jnp
from jax import lax
from jax.experimental import pallas as pl
from jax.experimental.pallas import tpu as pltpu
from jax.sharding import PartitionSpec as P

MESH = pl.DeviceIdType.MESH
F32 = jnp.float32
BF16 = jnp.bfloat16
I32 = jnp.int32
NEG = 32
BLOCK_ROWS = 128
QH = 8
PAIRS = QH * NEG
K0 = math.sqrt(2.0 / math.pi)
K1 = 0.044715


def iota(shape, axis):
    return lax.broadcasted_iota(I32, shape, axis)


def dot(a, b, ca=1, cb=0):
    return lax.dot_general(a, b, (((ca,), (cb,)), ((), ())), preferred_element_type=F32)


def fold(rows):
    w = rows.shape[1] // 2
    return jnp.concatenate([rows[:, :w], rows[:, w:]], axis=0)


def unfold(rows):
    return jnp.concatenate([rows[:QH], rows[QH:]], axis=1)


def kernel(
    dims,
    in_hbm, pos_hbm, nb_hbm, nr_hbm, mg_hbm, home_hbm, bank_hbm, up_hbm, bias_hbm, down_hbm,
    gi_ref, gd_ref,
    in_ref, pos_ref, nb_ref, nr_ref, mg_ref, home_ref, bank_ref, up_ref, bias_ref, down_ref,
    meta_all, e_all, ps_all, h_two, ht_send, ht_all, f_all, gd_all,
    xs, xr, xs2, xr2, xg, in_l, pos_l, dgelu,
    pm_sc, near_sc, q_sc, m_sc,
    g_own, g_send, gc_recv, gy_send, gy_recv, gz_send, gz_recv,
    r_own, r_send, rc_recv, ry_send, ry_recv, rz_send, rz_recv,
    p_sc, pz_recv,
    lsem, xsem, zsem, ysem, csem,
):
    nx, ny, nz, nc, cap = dims
    per = min(4, nz)
    chunks = nz // per
    rings = ny * per
    block = nc * rings
    slots = cap * block
    b = lax.axis_index("bank")
    x = lax.axis_index("head")
    c = lax.rem(b, nc)
    z = lax.rem(b // nc, nz)
    y = b // (nc * nz)
    oc = 1 - c
    width = in_ref.shape[1]
    half = width // 2
    units = up_ref.shape[1]
    rows_own = bank_ref.shape[0]
    homes = home_ref.shape[1]
    gd_pieces = units // ny // 16
    offs = [(s + 1) // 2 if s % 2 else -(s // 2) for s in range(nz)]

    def bid(yy, zz, cc):
        return (yy * nz + zz) * nc + cc

    def zat(off):
        return lax.rem(z + (off + nz), nz)

    def xdev(d):
        return (b, lax.rem(x + d, nx))

    def xcdev(d):
        return (bid(y, z, oc), lax.rem(x + d, nx))

    def zdev(off):
        return (bid(y, zat(off), c), x)

    def ydev(d):
        return (bid(lax.rem(y + d, ny), z, c), x)

    def piece_of(zz):
        return zz * gd_pieces // nz

    def owns(zz):
        return piece_of(zz + 1) > piece_of(zz)

    ys = sorted(range(1, ny), key=lambda d: -min(d, ny - d))
    xsd = sorted(range(1, nx), key=lambda d: -min(d, nx - d))
    cdev = xcdev(0)
    unsent = []

    def copy(src, dst, sems, i, dev):
        return pltpu.make_async_remote_copy(
            src_ref=src, dst_ref=dst, send_sem=sems.at[0, i], recv_sem=sems.at[1, i],
            device_id=dev, device_id_type=MESH,
        )

    def start(cp, when=None):
        if when is None:
            cp.start()
        else:
            pl.when(when)(cp.start)
        unsent.append((cp, when))

    def drain(count):
        for cp, when in unsent[:count]:
            if when is None:
                cp.wait_send()
            else:
                pl.when(when)(cp.wait_send)
        del unsent[:count]

    def zcopy(k, s, off, src, dst):
        return copy(src, dst, zsem, k * nz + s, zdev(off))

    def ycopy(k, d, src, dst):
        return copy(src, dst, ysem, k * ny + d, ydev(d))

    def ccopy(k, src, dst):
        return copy(src, dst, csem, k, cdev)

    def xcopy(k, d, src, dst):
        return copy(src, dst, xsem, k * nx + d, xdev(d))

    pairs = [
        (in_hbm, in_ref), (up_hbm, up_ref), (bias_hbm, bias_ref), (down_hbm, down_ref),
        (nb_hbm, nb_ref), (nr_hbm, nr_ref), (mg_hbm, mg_ref), (home_hbm, home_ref),
        (pos_hbm, pos_ref), (bank_hbm, bank_ref),
    ]
    loads = [pltpu.make_async_copy(src, dst, lsem.at[i]) for i, (src, dst) in enumerate(pairs)]
    for cp in loads:
        cp.start()

    barrier = pltpu.get_barrier_semaphore()
    greet = [xcdev(d) for d in range(nx)] + [xdev(d) for d in range(1, nx)]
    greet += [ydev(d) for d in range(1, ny)] + []
    greet = [zdev(o) for o in offs[:0:-1]] + greet
    for dev in greet:
        pl.semaphore_signal(barrier, inc=1, device_id=dev, device_id_type=MESH)

    for cp in loads[:4]:
        cp.wait()
    queries = in_ref[...]
    pre = dot(queries, up_ref[...]) + bias_ref[...].reshape(1, units)
    t = jnp.tanh(K0 * (pre + K1 * (pre * pre * pre)))
    hid = (0.5 * pre * (1.0 + t)).astype(BF16)
    h_two[0] = hid
    partial = dot(hid, down_ref[...])
    for i in range(nx):
        xs[i] = fold(partial[QH * i:QH * (i + 1)]).astype(BF16)

    for cp in loads[4:8]:
        cp.wait()
    mine8 = pl.ds(pl.multiple_of(x * QH, QH), QH)
    lanes = 128 // NEG

    def row_of(rows, i):
        return jnp.concatenate([rows[lanes * i + k:lanes * i + k + 1] for k in range(lanes)], axis=1)

    home = home_ref[...]
    part = iota((8, homes), 0)
    home8 = jnp.broadcast_to(home, (8, homes))
    table = jnp.where(part == 0, home8 >> 1, jnp.where(part == 1, home8 & 1, 0))
    table = table.astype(F32).astype(BF16)
    nb8, nr8, mg8 = nb_ref[mine8, :], nr_ref[mine8, :], mg_ref[mine8, :]
    for i in range(PAIRS // 128):
        hot = jnp.where(iota((homes, 128), 0) == row_of(nb8, i), 1.0, 0.0).astype(BF16)
        found = dot(table, hot)
        place = 2.0 * found[0:1] + found[1:2]
        ids = place * float(BLOCK_ROWS) + row_of(nr8, i).astype(F32)
        meta_all[0, 0, :, pl.ds(128 * i, 128)] = ids
        meta_all[0, 0, :, pl.ds(PAIRS + 128 * i, 128)] = row_of(mg8, i)

    pl.semaphore_wait(barrier, len(greet))

    far_first = list(range(nz - 1, 0, -1))

    def zgather(k, s, ref):
        return zcopy(k, s, -offs[s], ref.at[0, pl.ds(0, 1)], ref.at[s // per, pl.ds(s % per, 1)])

    for d in xsd:
        start(xcopy(0, d, xs.at[lax.rem(x + d, nx)], xr.at[d]))
    for s in far_first:
        start(zgather(0, s, meta_all))
    start(ccopy(0, h_two.at[0], h_two.at[1]))
    dgelu[...] = 0.5 * (1.0 + t) + 0.5 * pre * (1.0 - t * t) * (K0 * (1.0 + 3.0 * K1 * (pre * pre)))
    inf = queries.astype(F32)
    loads[8].wait()
    posf = pos_ref[...].astype(F32)
    for i in range(nx):
        in_l[i] = fold(inf[QH * i:QH * (i + 1)])
        pos_l[i] = fold(posf[QH * i:QH * (i + 1)])

    total = xs[x].astype(F32)
    for d in range(1, nx):
        xcopy(0, d, xs.at[0], xr.at[d]).wait_recv()
        total = total + xr[d].astype(F32)
    emb = (in_l[x] + total).astype(BF16)
    e_all[0, 0] = emb
    s16 = jnp.sum(emb.astype(F32) * pos_l[x], axis=1, keepdims=True)
    s8 = s16[:QH] + s16[QH:]
    diag = iota((QH, 128), 0) == iota((QH, 128), 1)
    ps_all[0, 0] = jnp.sum(jnp.where(diag, s8, 0.0), axis=0, keepdims=True)
    for s in range(1, nz):
        start(zgather(1, s, e_all))
    for s in range(1, nz):
        start(zgather(2, s, ps_all))

    def near_ring(ref, k, d=0):
        return ref.at[k, pl.ds(d * per, per)]

    def emb_z(k):
        for s in range(max(1, k * per), (k + 1) * per):
            zgather(1, s, e_all).wait_recv()
            zgather(2, s, ps_all).wait_recv()
        for d in ys:
            start(ycopy(2 + k, d, near_ring(e_all, k), near_ring(e_all, k, ny - d)))
            start(ycopy(6 + k, d, near_ring(ps_all, k), near_ring(ps_all, k, ny - d)))

    def emb_y(k):
        for d in range(1, ny):
            ycopy(2 + k, d, near_ring(e_all, k), near_ring(e_all, k, ny - d)).wait_recv()
            ycopy(6 + k, d, near_ring(ps_all, k), near_ring(ps_all, k, ny - d)).wait_recv()
        start(emb_core(2 + k, e_all, k))
        start(emb_core(6 + k, ps_all, k))

    def emb_core(i, ref, k):
        return ccopy(i, ref.at[k, pl.ds(0, rings)], ref.at[k, pl.ds(rings, rings)])

    for s in range(1, nz):
        zgather(0, s, meta_all).wait_recv()

    def meta_y(d):
        return ycopy(
            1, d, meta_all.at[:, pl.ds(0, per)], meta_all.at[:, pl.ds((ny - d) * per, per)]
        )

    for d in ys:
        start(meta_y(d))
    for d in range(1, ny):
        meta_y(d).wait_recv()
    meta_c = ccopy(1, meta_all.at[:, pl.ds(0, rings)], meta_all.at[:, pl.ds(rings, rings)])
    start(meta_c)
    emb_z(0)
    meta_c.wait_recv()
    loads[9].wait()

    tri = jnp.where(iota((PAIRS, PAIRS), 0) <= iota((PAIRS, PAIRS), 1), 1.0, 0.0).astype(BF16)
    q_lane = (iota((block, PAIRS), 1) // NEG + 1).astype(F32)
    def find(k):
        ids = meta_all[k, :, 0, pl.ds(0, PAIRS)].astype(I32)
        margins = meta_all[k, :, 0, pl.ds(PAIRS, PAIRS)]
        owner = ids // rows_own
        local = (ids - owner * rows_own).astype(F32)
        mine = owner == b
        prefix = dot(jnp.where(mine, 1.0, 0.0).astype(BF16), tri)
        pm = jnp.where(mine, prefix, 0.0)
        pm_sc[k] = pm
        rows, qs, ms = [], [], []
        for r in range(cap):
            sel = pm == float(r + 1)
            rows.append(jnp.sum(jnp.where(sel, local, 0.0), axis=1, keepdims=True))
            qs.append(jnp.sum(jnp.where(sel, q_lane, 0.0), axis=1, keepdims=True))
            ms.append(jnp.sum(jnp.where(sel, margins, 0.0), axis=1, keepdims=True))
        rows, qs = jnp.concatenate(rows, axis=0), jnp.concatenate(qs, axis=0)
        q_sc[k] = qs
        m_sc[k] = jnp.concatenate(ms, axis=0)
        row_i = jnp.where(qs > 0.5, rows, -1.0).astype(I32)
        hot_row = jnp.where(iota((slots, rows_own), 1) == row_i, 1.0, 0.0).astype(BF16)
        near_sc[k] = dot(hot_row, bank_ref[...]).astype(BF16)

    ind = jnp.where(iota((PAIRS, 128), 0) // NEG == iota((PAIRS, 128), 1), 1.0, 0.0).astype(BF16)

    def score(k):
        emb_core(2 + k, e_all, k).wait_recv()
        emb_core(6 + k, ps_all, k).wait_recv()
        qs = q_sc[k]
        q_i = qs.astype(I32) - 1
        ps_rep = jnp.concatenate([ps_all[k, :, 0, :]] * cap, axis=0)
        ps = jnp.sum(jnp.where(iota((slots, 128), 1) == q_i, ps_rep, 0.0), axis=1, keepdims=True)
        offsets = (ps - m_sc[k]).astype(BF16).astype(F32)
        group_i = lax.rem(iota((slots, 1), 0), block)
        target = jnp.where(qs > 0.5, group_i * 16 + q_i, -100)
        target = jnp.concatenate([target, target + QH], axis=0)
        hot_q = jnp.where(iota((2 * slots, block * 16), 1) == target, 1.0, 0.0).astype(BF16)
        embs = dot(hot_q, e_all[k].reshape(block * 16, half))
        near = near_sc[k].astype(F32)
        found = jnp.sum(
            embs[:slots] * near[:, :half] + embs[slots:] * near[:, half:], axis=1, keepdims=True
        )
        residual = offsets - found
        weighted = (residual * near).astype(BF16)
        weighted = jnp.concatenate([weighted[:, :half], weighted[:, half:]], axis=0)
        summed = dot(hot_q, weighted, 0, 0).reshape(block, 16, half)
        rounded = residual.astype(BF16).astype(F32)
        pm = pm_sc[k]
        per_pair = jnp.zeros((block, PAIRS), F32)
        for r in range(cap):
            per_pair = per_pair + jnp.where(
                pm == float(r + 1), rounded[r * block:(r + 1) * block], 0.0
            )
        rsum = dot(per_pair.astype(BF16), ind)
        g_send[k] = summed[rings:].astype(BF16)
        r_send[k, :, 0, :] = rsum[rings:]
        start(ccopy(10 + k, g_send.at[k], gc_recv.at[k]))
        start(ccopy(14 + k, r_send.at[k], rc_recv.at[k]))
        g_own[k] = summed[:rings]
        r_own[k, :, 0, :] = rsum[:rings]

    def sum_core(k):
        ccopy(10 + k, g_send.at[k], gc_recv.at[k]).wait_recv()
        ccopy(14 + k, r_send.at[k], rc_recv.at[k]).wait_recv()
        for d in ys + [0]:
            at = pl.ds(d * per, per)
            g_sum = g_own[k, at] + gc_recv[k, at].astype(F32)
            r_sum = r_own[k, at] + rc_recv[k, at]
            if d:
                gy_send[k, d] = g_sum.astype(BF16)
                ry_send[k, d] = r_sum
                start(ycopy(10 + k, d, gy_send.at[k, d], gy_recv.at[k, d]))
                start(ycopy(14 + k, d, ry_send.at[k, d], ry_recv.at[k, d]))
            else:
                g_own[k, at] = g_sum
                r_own[k, at] = r_sum

    def sum_y(k):
        g_sum = g_own[k, pl.ds(0, per)]
        r_sum = r_own[k, pl.ds(0, per)]
        for d in range(1, ny):
            ycopy(10 + k, d, gy_send.at[k, d], gy_recv.at[k, d]).wait_recv()
            ycopy(14 + k, d, ry_send.at[k, d], ry_recv.at[k, d]).wait_recv()
            g_sum = g_sum + gy_recv[k, d].astype(F32)
            r_sum = r_sum + ry_recv[k, d]
        gz_send[k] = g_sum.astype(BF16)
        rz_send[k] = r_sum
        if k == 0:
            g_own[0, 0] = g_sum[0]
        for s in range((k + 1) * per - 1, max(1, k * per) - 1, -1):
            start(zcopy(3, s, offs[s], gz_send.at[k, s % per], gz_recv.at[s]))
            start(zcopy(4, s, offs[s], rz_send.at[k, s % per], rz_recv.at[s]))

    if chunks == 4:
        order = [
            ("f", 0), ("f", 1), ("z", 1), ("y", 0), ("f", 2), ("z", 2), ("y", 1), ("s", 0),
            ("f", 3), ("s", 1), ("c", 0), ("z", 3), ("y", 2), ("c", 1), ("s", 2), ("a", 0),
            ("y", 3), ("c", 2), ("a", 1), ("s", 3), ("a", 2), ("c", 3), ("a", 3),
        ]
    else:
        order = [(name, k) for name in "fzysca" for k in range(chunks) if name + str(k) != "z0"]
    does = {"f": find, "z": emb_z, "y": emb_y, "s": score, "c": sum_core, "a": sum_y}
    for name, k in order:
        does[name](k)

    ccopy(0, h_two.at[0], h_two.at[1]).wait_recv()
    turned = jnp.concatenate([h_two[0].astype(F32), h_two[1].astype(F32)], axis=0).T
    ht_send[...] = turned.astype(BF16).reshape(ht_send.shape)
    for d in ys:
        start(ycopy(0, d, ht_send.at[lax.rem(y + d, ny)], ht_all.at[ny - d]))
    ht_all[0] = ht_send[y]

    wsum = g_own[0, 0]
    rsum = rz_send[0, 0]
    for s in range(1, nz):
        zcopy(3, s, offs[s], gz_send.at[0, 0], gz_recv.at[s]).wait_recv()
        zcopy(4, s, offs[s], rz_send.at[0, 0], rz_recv.at[s]).wait_recv()
        wsum = wsum + gz_recv[s].astype(F32)
        rsum = rsum + rz_recv[s]
    lane_q = iota((16, 128), 1) == lax.rem(iota((16, 128), 0), QH)
    rcol = jnp.sum(jnp.where(lane_q, rsum, 0.0), axis=1, keepdims=True)
    gradient = 2.0 * pos_l[x] * rcol - 2.0 * wsum
    xg[0, x] = gradient.astype(BF16)
    for d in xsd:
        start(xcopy(1, d, xg.at[0, x], xg.at[0, x]))
    for d in range(nx):
        start(copy(xg.at[0, x], xg.at[1, x], xsem, 3 * nx + d, xcdev(d)))
    for d in range(nx):
        src = lax.rem(x + nx - d, nx)
        if d:
            xcopy(1, d, xg.at[0, x], xg.at[0, src]).wait_recv()
        copy(xg.at[0, x], xg.at[1, src], xsem, 3 * nx + d, xcdev(d)).wait_recv()

    def halves(cr):
        pieces = [xg[cr, i].astype(F32) for i in range(nx)]
        top = jnp.concatenate([p[:QH] for p in pieces], axis=0)
        low = jnp.concatenate([p[QH:] for p in pieces], axis=0)
        f_all[0, cr] = jnp.where(c == 0, top, low).astype(BF16)
        return top, low

    top, low = halves(0)
    halves(1)
    for d in ys:
        start(ycopy(18, d, f_all.at[0], f_all.at[ny - d]))

    older = len(unsent)
    down_sum = dot(ht_all[0], f_all[0].reshape(nc * nx * QH, half))
    for d in range(1, ny):
        ycopy(0, d, ht_send.at[0], ht_all.at[ny - d]).wait_recv()
        ycopy(18, d, f_all.at[0], f_all.at[ny - d]).wait_recv()
        down_sum = down_sum + dot(ht_all[ny - d], f_all[ny - d].reshape(nc * nx * QH, half))
    p_sc[...] = down_sum.astype(BF16).reshape(gd_pieces, 16, half)
    for s in far_first:
        zz = zat(offs[s])
        start(zcopy(5, s, offs[s], p_sc.at[piece_of(zz)], pz_recv.at[s]), owns(zz))

    grad_all = jnp.concatenate([top, low], axis=1).astype(BF16)
    hidden_grad = dot(grad_all, down_ref[...], 1, 1)
    pre_grad = (hidden_grad * dgelu[...]).astype(BF16)
    carried = dot(pre_grad, up_ref[...], 1, 1)
    for i in range(nx):
        xs2[i] = fold(carried[QH * i:QH * (i + 1)]).astype(BF16)
    for d in xsd:
        start(xcopy(2, d, xs2.at[lax.rem(x + d, nx)], xr2.at[d]))

    drain(older)
    busy = owns(z)
    scale = 1.0 / math.sqrt(nx * QH * ny * nz * nc)

    @pl.when(busy)
    def _():
        acc = p_sc[piece_of(z)].astype(F32)
        for s in range(1, nz):
            zcopy(5, s, offs[s], p_sc.at[0], pz_recv.at[s]).wait_recv()
            acc = acc + pz_recv[s].astype(F32)
        gd_all[0, 0] = (acc * scale).astype(BF16)

    def zlast(s):
        return zgather(6, s, gd_all)

    for s in range(1, nz):
        start(zlast(s), busy)

    drain(len(unsent) - (nz - 1))

    carry = xs2[x].astype(F32) + gradient
    for d in range(1, nx):
        xcopy(2, d, xs2.at[0], xr2.at[d]).wait_recv()
        carry = carry + xr2[d].astype(F32)
    gi_ref[...] = unfold(carry).astype(BF16)

    def last_z(k):
        for s in range(max(1, k * per), (k + 1) * per):
            pl.when(owns(zat(offs[s])))(zlast(s).wait_recv)
        for d in ys:
            start(ycopy(19 + k, d, near_ring(gd_all, k), near_ring(gd_all, k, ny - d)))

    def last_y(k):
        for d in range(1, ny):
            ycopy(19 + k, d, near_ring(gd_all, k), near_ring(gd_all, k, ny - d)).wait_recv()
        start(emb_core(18 + k, gd_all, k))
        put(k, 0)

    def put(k, cr):
        at = c if cr == 0 else oc
        for s in range(per):
            zz = zat(offs[k * per + s])

            @pl.when(owns(zz))
            def _():
                for d in range(ny):
                    yy = lax.rem(y + d, ny)
                    row = pl.multiple_of((yy * gd_pieces + piece_of(zz)) * 16, 16)
                    col = pl.multiple_of(at * half, 128)
                    gd_ref[pl.ds(row, 16), pl.ds(col, half)] = gd_all[k, cr * rings + d * per + s]

    def last_core(k):
        emb_core(18 + k, gd_all, k).wait_recv()
        put(k, 1)

    stages = [last_z, last_y, last_core]
    for step in range(chunks + len(stages) - 1):
        for late, stage in enumerate(stages):
            if 0 <= step - late < chunks:
                stage(step - late)

    drain(len(unsent))


def on_device(
    dims, inputs, positives, margins, neg_block, neg_row, block_home, bank, up_weight, up_bias,
    down_weight,
):
    nx, ny, nz, nc, cap = dims
    width = inputs.shape[1]
    half = width // 2
    units = up_weight.shape[1]
    queries = inputs.shape[0]
    per = min(4, nz)
    chunks = nz // per
    rings = ny * per
    block = nc * rings
    slots = cap * block
    gd_pieces = units // ny // 16
    V = pltpu.VMEM
    args = (
        inputs, positives, neg_block, neg_row, margins, block_home.reshape(1, -1), bank,
        up_weight, up_bias, down_weight,
    )
    scratch = [V(a.shape, a.dtype) for a in args] + [
        V((chunks, block, 1, 2 * PAIRS), F32),
        V((chunks, block, 16, half), BF16),
        V((chunks, block, 1, 128), F32),
        V((nc, queries, units), BF16),
        V((ny, units // ny, nc * queries), BF16),
        V((ny, units // ny, nc * queries), BF16),
        V((ny, nc, queries, half), BF16),
        V((chunks, block, 16, half), BF16),
        V((nx, 16, half), BF16),
        V((nx, 16, half), BF16),
        V((nx, 16, half), BF16),
        V((nx, 16, half), BF16),
        V((nc, nx, 16, half), BF16),
        V((nx, 16, half), F32),
        V((nx, 16, half), F32),
        V((queries, units), F32),
        V((chunks, block, PAIRS), F32),
        V((chunks, slots, width), BF16),
        V((chunks, slots, 1), F32),
        V((chunks, slots, 1), F32),
        V((chunks, rings, 16, half), F32),
        V((chunks, rings, 16, half), BF16),
        V((chunks, rings, 16, half), BF16),
        V((chunks, ny, per, 16, half), BF16),
        V((chunks, ny, per, 16, half), BF16),
        V((chunks, per, 16, half), BF16),
        V((nz, 16, half), BF16),
        V((chunks, rings, 1, 128), F32),
        V((chunks, rings, 1, 128), F32),
        V((chunks, rings, 1, 128), F32),
        V((chunks, ny, per, 1, 128), F32),
        V((chunks, ny, per, 1, 128), F32),
        V((chunks, per, 1, 128), F32),
        V((nz, 1, 128), F32),
        V((gd_pieces, 16, half), BF16),
        V((nz, 16, half), BF16),
        pltpu.SemaphoreType.DMA((len(args),)),
        pltpu.SemaphoreType.DMA((2, 4 * nx)),
        pltpu.SemaphoreType.DMA((2, 7 * nz)),
        pltpu.SemaphoreType.DMA((2, 23 * ny)),
        pltpu.SemaphoreType.DMA((2, 22)),
    ]
    vmem = pl.BlockSpec(memory_space=pltpu.VMEM)
    return pl.pallas_call(
        functools.partial(kernel, dims),
        out_shape=(
            pltpu.VMEM((QH, width), BF16),
            pltpu.VMEM((units, width), BF16),
        ),
        in_specs=[pl.BlockSpec(memory_space=pltpu.HBM)] * len(args),
        out_specs=(vmem, vmem),
        scratch_shapes=scratch,
        compiler_params=pltpu.CompilerParams(
            collective_id=0, has_side_effects=True, vmem_limit_bytes=60 * 1024 * 1024
        ),
        cost_estimate=pl.CostEstimate(
            flops=4_000_000_000, bytes_accessed=6_000_000, transcendentals=30_000
        ),
    )(*args)


def solution(mesh, ny=4, nc=2, cap=4):
    nx = mesh.shape["head"]
    nz = mesh.shape["bank"] // (ny * nc)
    return jax.shard_map(
        functools.partial(on_device, (nx, ny, nz, nc, cap)),
        mesh=mesh,
        in_specs=(
            P("bank", None),
            P("bank", None),
            P("bank", None),
            P("bank", None),
            P("bank", None),
            P(),
            P("bank", None),
            P(None, "head"),
            P("head"),
            P("head", None),
        ),
        out_specs=(P(("bank", "head"), None), P("head", None)),
        check_vma=False,
    )
```
